32 devices in a mesh: replica: 2 (over x), req: 16 (over z, y, core).
Axes of the slice: x: 2, y: 2, z: 4, core: 2. Of those that a mesh axis runs over, the one named last changes fastest.
Arguments:
- residual_rows: bfloat16 [8192, 8192], P(('replica', 'req')), parts along dimension 0, may hold values from -6 to 6
- attention_norm_gain: bfloat16 [8192], replicated, may hold values from 0.099609375 to 1.8984375
- value_base_weight: bfloat16 [8192, 512], replicated, may hold values from -0.0625 to 0.0625
- adapter_down_weight: bfloat16 [32, 8192, 64], P('req'), may hold values from -0.0625 to 0.0625
- adapter_up_weight: bfloat16 [32, 64, 512], P('req'), may hold values from -0.75 to 0.75
- adapter_storage_slot: int32 [64], P('replica'), parts along dimension 0, may hold values from 0 to 31, as said below
- request_adapter_index: int32 [8192], P(('replica', 'req')), parts along dimension 0, may hold values from 0 to 31, as said below
Outputs:
- values_out: bfloat16 [8192, 512], P(('replica', 'req')), parts along dimension 0
The draws below stay inside these ranges and needn't reach their ends.
There are 2 independent parts, one for each index of `replica`. The reference program is written for one: setup_inputs(seed, part) draws one part's arguments, and reference() takes and returns one part's arrays. A program takes and returns all parts, laid end to end along the dimension named above; an argument that names none is the same for every part. Nothing has to cross between parts.
Inputs may be any that keep to these rules, and one draw needn't show every extreme that they name: A permutation: adapter a lies in slot adapter_storage_slot[a], held by device slot // 2 of req as its (slot % 2)-th adapter. `request_adapter_index`: among the rows of one device, at most 32 name adapters held by one device, and in every device's rows some holder gets exactly 32.
All inputs are finite; a program needn't handle non-finite values.
Results may differ from the reference program's by a relative error of at most 0.0058.
Values may be sent and summed in bfloat16 or wider, within the bound.
A program may use at most 128 MiB of HBM per device.

```python
import jax
import jax.numpy as jnp
from jax import lax

MODEL_WIDTH = 8192
OUTPUT_HALF = 512
ADAPTER_RANK = 64
ADP_DEV = 2
ROWS_DEV = 256
TOKENS = 4096
ADAPTER_COUNT = 32


def storage_order(key):
    return jax.random.permutation(jax.random.fold_in(key, 11), ADAPTER_COUNT).astype(jnp.int32)


def draw_adapter_storage_slot(key, part):
    return storage_order(key)


def draw_request_adapter_index(key, part):
    order = storage_order(key)
    key = jax.random.fold_in(key, 5)
    blocks = TOKENS // ROWS_DEV
    limit = 2 * ROWS_DEV // blocks

    def block_draw(sub):
        first, second, third, fourth = jax.random.split(sub, 4)
        busiest = jax.random.randint(first, (), 0, blocks)
        holders = jnp.arange(blocks * limit, dtype=jnp.int32) // limit
        scores = jax.random.randint(second, (blocks * limit,), 0, 1 << 20)
        scores = jnp.where(holders == busiest, -1, scores)
        chosen = holders[jnp.argsort(scores, stable=True)[:ROWS_DEV]]
        chosen = jax.random.permutation(third, chosen)
        within = jax.random.randint(fourth, (ROWS_DEV,), 0, ADP_DEV)
        return chosen * ADP_DEV + within
    storage_slots = jax.vmap(block_draw)(jax.random.split(key, blocks)).reshape(-1)
    inverse = jnp.argsort(order)
    return inverse[storage_slots].astype(jnp.int32)


def steps_of(stream_key, extent, cuts, least, top_value):
    factor_of, own = 1.0, jax.random.fold_in(stream_key, 6)
    for axis_at, parts in cuts:
        draws = jnp.exp(jax.random.uniform(jax.random.fold_in(own, axis_at), (parts,), jnp.float32, least / len(cuts), top_value / len(cuts)))
        factor_of = factor_of * jnp.repeat(draws, extent[axis_at] // parts).reshape([-1 if axis == axis_at else 1 for axis in range(len(extent))])
    return factor_of


def centred(rng, shape, width, most, shards=(), held_as=jnp.bfloat16):
    entries = width * jax.random.normal(rng, shape, jnp.float32)
    if shards:
        entries = entries * steps_of(rng, shape, shards, -0.22, 0.18)
    return jnp.clip(entries, -most, most).astype(held_as)


def setup_inputs(seed: int = 0, part: int = 0) -> dict:
    arg_keys = jax.random.split(jax.random.key(seed), 8)
    part_splits = jax.random.split(jax.random.fold_in(arg_keys[7], part), 8)
    return {
        "residual_rows": centred(part_splits[0], (TOKENS, MODEL_WIDTH), 1.0, 6.0, ((0, 16),)),
        "attention_norm_gain": jnp.clip(1.0 + 0.18 * jax.random.normal(arg_keys[1], (MODEL_WIDTH,), jnp.float32), 0.099609375, 1.8984375).astype(jnp.bfloat16),
        "value_base_weight": centred(arg_keys[2], (MODEL_WIDTH, OUTPUT_HALF), MODEL_WIDTH ** -0.5, 0.0625),
        "adapter_down_weight": centred(arg_keys[3], (ADAPTER_COUNT, MODEL_WIDTH, ADAPTER_RANK), MODEL_WIDTH ** -0.5, 0.0625, ((0, 16),)),
        "adapter_up_weight": centred(arg_keys[4], (ADAPTER_COUNT, ADAPTER_RANK, OUTPUT_HALF), ADAPTER_RANK ** -0.5, 0.75, ((0, 16),)),
        "adapter_storage_slot": draw_adapter_storage_slot(jax.random.fold_in(jax.random.fold_in(arg_keys[7], part), 71), part),
        "request_adapter_index": draw_request_adapter_index(jax.random.fold_in(jax.random.fold_in(arg_keys[7], part), 71), part),
    }


def reference(residual_rows, attention_norm_gain, value_base_weight, adapter_down_weight, adapter_up_weight, adapter_storage_slot, request_adapter_index):
    wide = residual_rows.astype(jnp.float32)
    factor = lax.rsqrt(lax.optimization_barrier(jnp.mean(wide * wide, axis=-1, keepdims=True)) + 1e-05)
    normed = (wide * factor * attention_norm_gain.astype(jnp.float32)).astype(jnp.bfloat16)
    base = jnp.dot(normed, value_base_weight, preferred_element_type=jnp.float32)
    slot = adapter_storage_slot[request_adapter_index].astype(jnp.int32)
    blocked_rows = normed.reshape(-1, 16, normed.shape[1])
    blocked_slots = slot.reshape(-1, 16)

    def one_block(pair):
        rows, storage_slots = pair
        down_product = adapter_down_weight[storage_slots].astype(jnp.float32)
        rank_reduced = jnp.einsum('bd,bdr->br', rows.astype(jnp.float32), down_product).astype(jnp.bfloat16)
        upper_product = adapter_up_weight[storage_slots].astype(jnp.float32)
        return jnp.einsum('br,bro->bo', rank_reduced.astype(jnp.float32), upper_product).astype(jnp.bfloat16)
    delta = lax.map(one_block, (blocked_rows, blocked_slots)).reshape(base.shape)
    return (base + delta.astype(jnp.float32)).astype(jnp.bfloat16)
```

```python
import functools

import jax
import jax.numpy as jnp
from jax import lax
from jax.experimental import pallas as pl
from jax.experimental.pallas import tpu as pltpu
from jax.sharding import PartitionSpec as P

MESH = pl.DeviceIdType.MESH
PLANE = 8


def kernel(
    replicas,
    inner,
    planes,
    stored,
    rank,
    x_hbm,
    gain_ref,
    base_w_hbm,
    down_hbm,
    slot_ref,
    base_ref,
    sum_ref,
    x_v,
    w_v,
    down_buf,
    rows_buf,
    slot_buf,
    acc,
    part_buf,
    down_recv,
    up_send,
    dn_send,
    plane_send,
    rows_send,
    rows_recv,
    slot_send,
    slot_recv,
    part_send,
    part_recv,
    local_sem,
):
    r = lax.axis_index("replica")
    q = lax.axis_index("req")
    z = q // inner
    i = q % inner
    e = r * inner + i
    rows = x_hbm.shape[0]
    width = x_hbm.shape[1] // PLANE
    cols = stored * rank

    def peer(k):
        e2 = lax.rem(e + k, PLANE)
        return e2, (e2 // inner, z * inner + lax.rem(e2, inner))

    has_up = z < planes - 1
    has_dn = z > 0
    above = (r, jnp.minimum(z + 1, planes - 1) * inner + i)
    below = (r, jnp.maximum(z - 1, 0) * inner + i)

    own_x = pltpu.make_async_copy(x_hbm, x_v, local_sem.at[0])
    own_w = pltpu.make_async_copy(base_w_hbm, w_v, local_sem.at[1])
    own_down = pltpu.make_async_copy(
        down_hbm.at[:, pl.ds(pl.multiple_of(e * width, width), width)],
        down_buf.at[z, i],
        local_sem.at[2],
    )
    own_down.start()
    own_x.start()

    barrier = pltpu.get_barrier_semaphore()
    for k in range(1, PLANE):
        pl.semaphore_signal(barrier, inc=1, device_id=peer(k)[1], device_id_type=MESH)

    @pl.when(has_up)
    def _():
        pl.semaphore_signal(barrier, inc=1, device_id=above, device_id_type=MESH)

    @pl.when(has_dn)
    def _():
        pl.semaphore_signal(barrier, inc=1, device_id=below, device_id_type=MESH)

    lines = jnp.where(has_up, 1, 0) + jnp.where(has_dn, 1, 0)
    pl.semaphore_wait(barrier, PLANE - 1 + lines)

    def plane_copy(k):
        i2 = lax.rem(i + k, inner)
        e2 = r * inner + i2
        return pltpu.make_async_remote_copy(
            src_ref=down_hbm.at[:, pl.ds(pl.multiple_of(e2 * width, width), width)],
            dst_ref=down_buf.at[z, i],
            send_sem=plane_send.at[k],
            recv_sem=down_recv.at[z, i],
            device_id=(r, z * inner + i2),
            device_id_type=MESH,
        )

    def rows_copy(k):
        e2, dev = peer(k)
        return pltpu.make_async_remote_copy(
            src_ref=x_hbm.at[:, pl.ds(pl.multiple_of(e2 * width, width), width)],
            dst_ref=rows_buf.at[e],
            send_sem=rows_send.at[k],
            recv_sem=rows_recv.at[e],
            device_id=dev,
            device_id_type=MESH,
        )

    def slot_copy(k):
        _, dev = peer(k)
        return pltpu.make_async_remote_copy(
            src_ref=slot_ref,
            dst_ref=slot_buf.at[e],
            send_sem=slot_send.at[k],
            recv_sem=slot_recv.at[e],
            device_id=dev,
            device_id_type=MESH,
        )

    def line_copy(b, j, up):
        return pltpu.make_async_remote_copy(
            src_ref=down_buf.at[b, j],
            dst_ref=down_buf.at[b, j],
            send_sem=(up_send if up else dn_send).at[b, j],
            recv_sem=down_recv.at[b, j],
            device_id=above if up else below,
            device_id_type=MESH,
        )

    def block_recv(b, j):
        pltpu.make_async_remote_copy(
            src_ref=down_buf.at[b, j],
            dst_ref=down_buf.at[b, j],
            send_sem=up_send.at[b, j],
            recv_sem=down_recv.at[b, j],
            device_id=above,
            device_id_type=MESH,
        ).wait_recv()

    def pass_on(b, j, up):
        @pl.when(has_up if up else has_dn)
        def _():
            line_copy(b, j, up).start()

    for k in range(1, inner):
        plane_copy(k).start()
    own_down.wait()
    pass_on(z, i, True)
    pass_on(z, i, False)
    for k in range(1, PLANE):
        slot_copy(k).start()
        rows_copy(k).start()
    own_w.start()
    slot_buf[e] = slot_ref[...]
    for k in range(1, inner):
        j = lax.rem(i + k, inner)
        block_recv(z, j)
        pass_on(z, j, True)
        pass_on(z, j, False)

    own_x.wait()
    square = jnp.zeros((rows, 1), jnp.float32)
    for c in range(PLANE):
        wide = x_v[:, c * width : (c + 1) * width].astype(jnp.float32)
        square += jnp.sum(wide * wide, axis=1, keepdims=True)
        x_v[:, c * width : (c + 1) * width] = (
            wide * gain_ref[c]
        ).astype(jnp.bfloat16)
    factor = lax.rsqrt(square / (width * PLANE) + 1e-05)
    own_w.wait()
    base_ref[...] = jnp.zeros_like(base_ref)

    def base_step(c):
        at = pl.multiple_of(c * width, width)
        base_ref[...] += jnp.dot(
            x_v[:, pl.ds(at, width)],
            w_v[pl.ds(at, width), :],
            preferred_element_type=jnp.float32,
        )

    pl.loop(0, PLANE)(base_step)
    base_ref[...] = base_ref[...] * factor
    factor_row = jnp.transpose(jnp.broadcast_to(factor, (rows, 128)))[0:1, :]

    def take(s, forward):
        low, high = z - s, z + s

        @pl.when(low >= 0)
        def _():
            @pl.loop(0, inner)
            def _(j):
                block_recv(low, j)
                if forward:
                    pass_on(low, j, True)

        @pl.when(high < planes)
        def _():
            @pl.loop(0, inner)
            def _(j):
                block_recv(high, j)
                if forward:
                    pass_on(high, j, False)

    gain_own = gain_ref[e]

    def multiply(b):
        down = down_buf[b].reshape(inner * cols, width)

        @pl.loop(0, PLANE)
        def _(n):
            product = lax.dot_general(
                down,
                rows_buf[n],
                (((1,), (1,)), ((), ())),
                preferred_element_type=jnp.float32,
            )
            slots = slot_buf[n][0:1, :]
            total = acc[n]
            for j in range(inner):
                for w in range(stored):
                    at = (j * stored + w) * rank
                    mine = slots == (b * inner + j) * stored + w
                    total = jnp.where(mine, product[at : at + rank], total)
            acc[n] = total

    @pl.loop(1, planes - 1)
    def _(s):
        take(s, True)

    own_rows = pltpu.make_async_copy(
        x_v.at[:, pl.ds(pl.multiple_of(e * width, width), width)],
        rows_buf.at[e],
        local_sem.at[3],
    )
    own_rows.start()
    acc[...] = jnp.zeros_like(acc)
    own_rows.wait()
    for k in range(1, PLANE):
        e2, dev = peer(k)
        pltpu.make_async_remote_copy(
            src_ref=slot_ref,
            dst_ref=slot_buf.at[e2],
            send_sem=slot_send.at[k],
            recv_sem=slot_recv.at[e2],
            device_id=dev,
            device_id_type=MESH,
        ).wait_recv()
        pltpu.make_async_remote_copy(
            src_ref=rows_buf.at[e2],
            dst_ref=rows_buf.at[e2],
            send_sem=rows_send.at[k],
            recv_sem=rows_recv.at[e2],
            device_id=dev,
            device_id_type=MESH,
        ).wait_recv()
        rows_buf[e2] = (rows_buf[e2].astype(jnp.float32) * gain_own).astype(jnp.bfloat16)

    multiply(z)

    @pl.loop(1, planes)
    def _(s):
        @pl.when(s == planes - 1)
        def _():
            take(s, False)

        @pl.when(z - s >= 0)
        def _():
            multiply(z - s)

        @pl.when(z + s < planes)
        def _():
            multiply(z + s)

    def part_copy(k):
        e2, dev = peer(k)
        return pltpu.make_async_remote_copy(
            src_ref=acc.at[e2],
            dst_ref=part_buf.at[e],
            send_sem=part_send.at[k],
            recv_sem=part_recv.at[e],
            device_id=dev,
            device_id_type=MESH,
        )

    for k in range(1, PLANE):
        part_copy(k).start()
    total = acc[e]
    for k in range(1, PLANE):
        e2, dev = peer(k)
        pltpu.make_async_remote_copy(
            src_ref=part_buf.at[e2],
            dst_ref=part_buf.at[e2],
            send_sem=part_send.at[k],
            recv_sem=part_recv.at[e2],
            device_id=dev,
            device_id_type=MESH,
        ).wait_recv()
        total += part_buf[e2]
    sum_ref[...] = total * factor_row

    for k in range(1, inner):
        plane_copy(k).wait_send()
    for k in range(1, PLANE):
        slot_copy(k).wait_send()
        rows_copy(k).wait_send()
        part_copy(k).wait_send()

    @pl.loop(0, planes)
    def _(b):
        @pl.when(jnp.logical_and(has_up, b <= z))
        def _():
            @pl.loop(0, inner)
            def _(j):
                line_copy(b, j, True).wait_send()

        @pl.when(jnp.logical_and(has_dn, b >= z))
        def _():
            @pl.loop(0, inner)
            def _(j):
                line_copy(b, j, False).wait_send()


def shards(
    residual_rows,
    attention_norm_gain,
    value_base_weight,
    adapter_down_weight,
    adapter_up_weight,
    adapter_storage_slot,
    request_adapter_index,
):
    replicas = lax.axis_size("replica")
    devices = lax.axis_size("req")
    inner = PLANE // replicas
    planes = devices // inner
    rows, features = residual_rows.shape
    width = features // PLANE
    stored, _, rank = adapter_down_weight.shape
    outputs = value_base_weight.shape[1]
    cols = stored * rank
    adapter_ids = jnp.arange(adapter_storage_slot.shape[0], dtype=jnp.int32)
    slot_hot = request_adapter_index[:, None] == adapter_ids[None, :]
    slot = jnp.sum(jnp.where(slot_hot, adapter_storage_slot[None, :], 0), axis=1)
    up = lax.all_gather(adapter_up_weight, "req", axis=0, tiled=True)
    down = jnp.transpose(adapter_down_weight, (0, 2, 1)).reshape(cols, features)
    gain = attention_norm_gain.astype(jnp.float32).reshape(PLANE, 1, width)
    anyspace = pl.BlockSpec(memory_space=pl.ANY)
    vmem = pl.BlockSpec(memory_space=pltpu.VMEM)
    dma = pltpu.SemaphoreType.DMA
    base, summed = pl.pallas_call(
        functools.partial(kernel, replicas, inner, planes, stored, rank),
        out_shape=(
            jax.ShapeDtypeStruct((rows, outputs), jnp.float32),
            jax.ShapeDtypeStruct((rank, rows), jnp.float32),
        ),
        in_specs=[anyspace, vmem, anyspace, anyspace, vmem],
        out_specs=(vmem, vmem),
        scratch_shapes=[
            pltpu.VMEM((rows, features), jnp.bfloat16),
            pltpu.VMEM((features, outputs), jnp.bfloat16),
            pltpu.VMEM((planes, inner, cols, width), jnp.bfloat16),
            pltpu.VMEM((PLANE, rows, width), jnp.bfloat16),
            pltpu.VMEM((PLANE, 8, rows), jnp.int32),
            pltpu.VMEM((PLANE, rank, rows), jnp.float32),
            pltpu.VMEM((PLANE, rank, rows), jnp.float32),
            dma((planes, inner)),
            dma((planes, inner)),
            dma((planes, inner)),
            dma((inner,)),
            dma((PLANE,)),
            dma((PLANE,)),
            dma((PLANE,)),
            dma((PLANE,)),
            dma((PLANE,)),
            dma((PLANE,)),
            dma((4,)),
        ],
        compiler_params=pltpu.CompilerParams(
            collective_id=0, has_side_effects=True, vmem_limit_bytes=56 * 1024 * 1024
        ),
        cost_estimate=pl.CostEstimate(
            flops=12 * 10**9, bytes_accessed=250 * 10**6, transcendentals=0
        ),
    )(
        residual_rows,
        gain,
        value_base_weight,
        down,
        jnp.broadcast_to(slot[None, :], (8, rows)),
    )
    shrink = jnp.transpose(summed).astype(jnp.bfloat16)
    slots = up.shape[0]
    mine = slot[:, None] == jnp.arange(slots, dtype=jnp.int32)[None, :]
    spread = jnp.where(mine[:, :, None], shrink[:, None, :], jnp.zeros((), jnp.bfloat16))
    delta = jnp.dot(
        spread.reshape(rows, slots * rank),
        up.reshape(slots * rank, outputs),
        preferred_element_type=jnp.float32,
    ).astype(jnp.bfloat16)
    return (base + delta.astype(jnp.float32)).astype(jnp.bfloat16)


def solution(mesh):
    return jax.shard_map(
        shards,
        mesh=mesh,
        in_specs=(
            P(("replica", "req"), None),
            P(),
            P(),
            P("req", None, None),
            P("req", None, None),
            P("replica"),
            P(("replica", "req")),
        ),
        out_specs=P(("replica", "req"), None),
        check_vma=False,
    )
```

```python
import functools

import jax
import jax.numpy as jnp
from jax import lax
from jax.experimental import pallas as pl
from jax.experimental.pallas import tpu as pltpu
from jax.sharding import PartitionSpec as P

MESH = pl.DeviceIdType.MESH
PLANE = 8


def kernel(
    replicas,
    inner,
    planes,
    stored,
    rank,
    x_hbm,
    gain_ref,
    base_w_hbm,
    down_hbm,
    up_ref,
    slot_ref,
    out_ref,
    base_ref,
    x_v,
    w_v,
    down_buf,
    up_buf,
    rows_buf,
    slot_buf,
    acc,
    part_buf,
    shrink_buf,
    answer,
    delta_buf,
    down_recv,
    small_recv,
    small_up,
    small_dn,
    small_plane,
    up_send,
    dn_send,
    plane_send,
    rows_send,
    rows_recv,
    slot_send,
    slot_recv,
    part_send,
    part_recv,
    shrink_send,
    shrink_recv,
    delta_send,
    delta_recv,
    local_sem,
):
    r = lax.axis_index("replica")
    q = lax.axis_index("req")
    z = q // inner
    i = q % inner
    e = r * inner + i
    rows = x_hbm.shape[0]
    width = x_hbm.shape[1] // PLANE
    cols = stored * rank

    def peer(k):
        e2 = lax.rem(e + k, PLANE)
        return e2, (e2 // inner, z * inner + lax.rem(e2, inner))

    has_up = z < planes - 1
    has_dn = z > 0
    above = (r, jnp.minimum(z + 1, planes - 1) * inner + i)
    below = (r, jnp.maximum(z - 1, 0) * inner + i)

    own_x = pltpu.make_async_copy(x_hbm, x_v, local_sem.at[0])
    own_w = pltpu.make_async_copy(base_w_hbm, w_v, local_sem.at[1])
    own_down = pltpu.make_async_copy(
        down_hbm.at[:, pl.ds(pl.multiple_of(e * width, width), width)],
        down_buf.at[z, i],
        local_sem.at[2],
    )
    own_down.start()
    own_x.start()

    barrier = pltpu.get_barrier_semaphore()
    for k in range(1, PLANE):
        pl.semaphore_signal(barrier, inc=1, device_id=peer(k)[1], device_id_type=MESH)

    @pl.when(has_up)
    def _():
        pl.semaphore_signal(barrier, inc=1, device_id=above, device_id_type=MESH)

    @pl.when(has_dn)
    def _():
        pl.semaphore_signal(barrier, inc=1, device_id=below, device_id_type=MESH)

    lines = jnp.where(has_up, 1, 0) + jnp.where(has_dn, 1, 0)
    pl.semaphore_wait(barrier, PLANE - 1 + lines)

    def plane_copy(k):
        i2 = lax.rem(i + k, inner)
        e2 = r * inner + i2
        return pltpu.make_async_remote_copy(
            src_ref=down_hbm.at[:, pl.ds(pl.multiple_of(e2 * width, width), width)],
            dst_ref=down_buf.at[z, i],
            send_sem=plane_send.at[k],
            recv_sem=down_recv.at[z, i],
            device_id=(r, z * inner + i2),
            device_id_type=MESH,
        )

    share = up_ref.shape[0] // PLANE

    def small_copy(k):
        i2 = lax.rem(i + k, inner)
        e2 = r * inner + i2
        return pltpu.make_async_remote_copy(
            src_ref=up_ref.at[pl.ds(pl.multiple_of(e2 * share, share), share)],
            dst_ref=up_buf.at[z, i],
            send_sem=small_plane.at[k],
            recv_sem=small_recv.at[z, i],
            device_id=(r, z * inner + i2),
            device_id_type=MESH,
        )

    def small_line(b, j, up):
        return pltpu.make_async_remote_copy(
            src_ref=up_buf.at[b, j],
            dst_ref=up_buf.at[b, j],
            send_sem=(small_up if up else small_dn).at[b, j],
            recv_sem=small_recv.at[b, j],
            device_id=above if up else below,
            device_id_type=MESH,
        )

    def rows_copy(k):
        e2, dev = peer(k)
        return pltpu.make_async_remote_copy(
            src_ref=x_hbm.at[:, pl.ds(pl.multiple_of(e2 * width, width), width)],
            dst_ref=rows_buf.at[e],
            send_sem=rows_send.at[k],
            recv_sem=rows_recv.at[e],
            device_id=dev,
            device_id_type=MESH,
        )

    def slot_copy(k):
        _, dev = peer(k)
        return pltpu.make_async_remote_copy(
            src_ref=slot_ref,
            dst_ref=slot_buf.at[e],
            send_sem=slot_send.at[k],
            recv_sem=slot_recv.at[e],
            device_id=dev,
            device_id_type=MESH,
        )

    def line_copy(b, j, up):
        return pltpu.make_async_remote_copy(
            src_ref=down_buf.at[b, j],
            dst_ref=down_buf.at[b, j],
            send_sem=(up_send if up else dn_send).at[b, j],
            recv_sem=down_recv.at[b, j],
            device_id=above if up else below,
            device_id_type=MESH,
        )

    def block_recv(b, j):
        pltpu.make_async_remote_copy(
            src_ref=down_buf.at[b, j],
            dst_ref=down_buf.at[b, j],
            send_sem=up_send.at[b, j],
            recv_sem=down_recv.at[b, j],
            device_id=above,
            device_id_type=MESH,
        ).wait_recv()
        small_line(b, j, True).wait_recv()

    def pass_on(b, j, up):
        @pl.when(has_up if up else has_dn)
        def _():
            line_copy(b, j, up).start()
            small_line(b, j, up).start()

    for k in range(1, inner):
        plane_copy(k).start()
        small_copy(k).start()
    up_buf[z, i] = up_ref[pl.ds(pl.multiple_of(e * share, share), share), :]
    own_down.wait()
    pass_on(z, i, True)
    pass_on(z, i, False)
    for k in range(1, PLANE):
        slot_copy(k).start()
        rows_copy(k).start()
    own_w.start()
    slot_buf[e] = slot_ref[...]
    for k in range(1, inner):
        j = lax.rem(i + k, inner)
        block_recv(z, j)
        pass_on(z, j, True)
        pass_on(z, j, False)

    own_x.wait()
    square = jnp.zeros((rows, 1), jnp.float32)
    for c in range(PLANE):
        wide = x_v[:, c * width : (c + 1) * width].astype(jnp.float32)
        square += jnp.sum(wide * wide, axis=1, keepdims=True)
        x_v[:, c * width : (c + 1) * width] = (
            wide * gain_ref[c]
        ).astype(jnp.bfloat16)
    factor = lax.rsqrt(square / (width * PLANE) + 1e-05)
    own_w.wait()
    base_ref[...] = jnp.zeros_like(base_ref)

    def base_step(c):
        at = pl.multiple_of(c * width, width)
        base_ref[...] += jnp.dot(
            x_v[:, pl.ds(at, width)],
            w_v[pl.ds(at, width), :],
            preferred_element_type=jnp.float32,
        )

    pl.loop(0, PLANE)(base_step)
    base_ref[...] = base_ref[...] * factor
    factor_row = jnp.transpose(jnp.broadcast_to(factor, (rows, 128)))[0:1, :]

    def take(s, forward):
        low, high = z - s, z + s

        @pl.when(low >= 0)
        def _():
            @pl.loop(0, inner)
            def _(j):
                block_recv(low, j)
                if forward:
                    pass_on(low, j, True)

        @pl.when(high < planes)
        def _():
            @pl.loop(0, inner)
            def _(j):
                block_recv(high, j)
                if forward:
                    pass_on(high, j, False)

    gain_own = gain_ref[e]

    def multiply(b):
        down = down_buf[b].reshape(inner * cols, width)

        @pl.loop(0, PLANE)
        def _(n):
            product = lax.dot_general(
                down,
                rows_buf[n],
                (((1,), (1,)), ((), ())),
                preferred_element_type=jnp.float32,
            )
            slots = slot_buf[n][0:1, :]
            total = acc[n]
            for j in range(inner):
                for w in range(stored):
                    at = (j * stored + w) * rank
                    mine = slots == (b * inner + j) * stored + w
                    total = jnp.where(mine, product[at : at + rank], total)
            acc[n] = total

    @pl.loop(1, planes - 1)
    def _(s):
        take(s, True)

    own_rows = pltpu.make_async_copy(
        x_v.at[:, pl.ds(pl.multiple_of(e * width, width), width)],
        rows_buf.at[e],
        local_sem.at[3],
    )
    own_rows.start()
    acc[...] = jnp.zeros_like(acc)
    own_rows.wait()
    for k in range(1, PLANE):
        e2, dev = peer(k)
        pltpu.make_async_remote_copy(
            src_ref=slot_ref,
            dst_ref=slot_buf.at[e2],
            send_sem=slot_send.at[k],
            recv_sem=slot_recv.at[e2],
            device_id=dev,
            device_id_type=MESH,
        ).wait_recv()
        pltpu.make_async_remote_copy(
            src_ref=rows_buf.at[e2],
            dst_ref=rows_buf.at[e2],
            send_sem=rows_send.at[k],
            recv_sem=rows_recv.at[e2],
            device_id=dev,
            device_id_type=MESH,
        ).wait_recv()
        rows_buf[e2] = (rows_buf[e2].astype(jnp.float32) * gain_own).astype(jnp.bfloat16)

    multiply(z)

    @pl.loop(1, planes)
    def _(s):
        @pl.when(s == planes - 1)
        def _():
            take(s, False)

        @pl.when(z - s >= 0)
        def _():
            multiply(z - s)

        @pl.when(z + s < planes)
        def _():
            multiply(z + s)

    def part_copy(k):
        e2, dev = peer(k)
        return pltpu.make_async_remote_copy(
            src_ref=acc.at[e2],
            dst_ref=part_buf.at[e],
            send_sem=part_send.at[k],
            recv_sem=part_recv.at[e],
            device_id=dev,
            device_id_type=MESH,
        )

    for k in range(1, PLANE):
        part_copy(k).start()
    total = acc[e]
    for k in range(1, PLANE):
        e2, dev = peer(k)
        pltpu.make_async_remote_copy(
            src_ref=part_buf.at[e2],
            dst_ref=part_buf.at[e2],
            send_sem=part_send.at[k],
            recv_sem=part_recv.at[e2],
            device_id=dev,
            device_id_type=MESH,
        ).wait_recv()
        total += part_buf[e2]
    shrink_buf[e] = (total * factor_row).astype(jnp.bfloat16)

    def shrink_copy(k):
        _, dev = peer(k)
        return pltpu.make_async_remote_copy(
            src_ref=shrink_buf.at[e],
            dst_ref=shrink_buf.at[e],
            send_sem=shrink_send.at[k],
            recv_sem=shrink_recv.at[e],
            device_id=dev,
            device_id_type=MESH,
        )

    def delta_copy(k):
        e2, dev = peer(k)
        return pltpu.make_async_remote_copy(
            src_ref=answer.at[e2],
            dst_ref=delta_buf.at[e],
            send_sem=delta_send.at[k],
            recv_sem=delta_recv.at[e],
            device_id=dev,
            device_id_type=MESH,
        )

    def expand(n):
        slots = slot_buf[n][0:1, :]
        shrunk = shrink_buf[n].astype(jnp.float32)

        def block(b, total):
            spread = jnp.concatenate(
                [
                    jnp.where(slots == b * inner * stored + a, shrunk, 0.0)
                    for a in range(inner * stored)
                ],
                axis=0,
            ).astype(jnp.bfloat16)
            for j in range(inner):
                total += jnp.dot(
                    up_buf[b, j],
                    spread[j * cols : (j + 1) * cols],
                    preferred_element_type=jnp.float32,
                )
            return total

        zero = jnp.zeros((share, rows), jnp.float32)
        return lax.fori_loop(0, planes, block, zero).astype(jnp.bfloat16)

    for k in range(1, PLANE):
        shrink_copy(k).start()
    delta_buf[e] = expand(e)
    for k in range(1, PLANE):
        e2, dev = peer(k)
        pltpu.make_async_remote_copy(
            src_ref=shrink_buf.at[e2],
            dst_ref=shrink_buf.at[e2],
            send_sem=shrink_send.at[k],
            recv_sem=shrink_recv.at[e2],
            device_id=dev,
            device_id_type=MESH,
        ).wait_recv()
        answer[e2] = expand(e2)
        delta_copy(k).start()
    for k in range(1, PLANE):
        e2, dev = peer(k)
        pltpu.make_async_remote_copy(
            src_ref=delta_buf.at[e2],
            dst_ref=delta_buf.at[e2],
            send_sem=delta_send.at[k],
            recv_sem=delta_recv.at[e2],
            device_id=dev,
            device_id_type=MESH,
        ).wait_recv()
    delta = delta_buf[...].reshape(PLANE * share, rows).astype(jnp.float32)
    out_ref[...] = (base_ref[...] + jnp.transpose(delta)).astype(jnp.bfloat16)

    for k in range(1, inner):
        plane_copy(k).wait_send()
        small_copy(k).wait_send()
    for k in range(1, PLANE):
        slot_copy(k).wait_send()
        rows_copy(k).wait_send()
        part_copy(k).wait_send()
        shrink_copy(k).wait_send()
        delta_copy(k).wait_send()

    @pl.loop(0, planes)
    def _(b):
        @pl.when(jnp.logical_and(has_up, b <= z))
        def _():
            @pl.loop(0, inner)
            def _(j):
                line_copy(b, j, True).wait_send()
                small_line(b, j, True).wait_send()

        @pl.when(jnp.logical_and(has_dn, b >= z))
        def _():
            @pl.loop(0, inner)
            def _(j):
                line_copy(b, j, False).wait_send()
                small_line(b, j, False).wait_send()


def shards(
    residual_rows,
    attention_norm_gain,
    value_base_weight,
    adapter_down_weight,
    adapter_up_weight,
    adapter_storage_slot,
    request_adapter_index,
):
    replicas = lax.axis_size("replica")
    devices = lax.axis_size("req")
    inner = PLANE // replicas
    planes = devices // inner
    rows, features = residual_rows.shape
    width = features // PLANE
    stored, _, rank = adapter_down_weight.shape
    outputs = value_base_weight.shape[1]
    cols = stored * rank
    adapter_ids = jnp.arange(adapter_storage_slot.shape[0], dtype=jnp.int32)
    slot_hot = request_adapter_index[:, None] == adapter_ids[None, :]
    slot = jnp.sum(jnp.where(slot_hot, adapter_storage_slot[None, :], 0), axis=1)
    up = jnp.transpose(adapter_up_weight, (2, 0, 1)).reshape(outputs, cols)
    down = jnp.transpose(adapter_down_weight, (0, 2, 1)).reshape(cols, features)
    gain = attention_norm_gain.astype(jnp.float32).reshape(PLANE, 1, width)
    anyspace = pl.BlockSpec(memory_space=pl.ANY)
    vmem = pl.BlockSpec(memory_space=pltpu.VMEM)
    dma = pltpu.SemaphoreType.DMA
    return pl.pallas_call(
        functools.partial(kernel, replicas, inner, planes, stored, rank),
        out_shape=jax.ShapeDtypeStruct((rows, outputs), jnp.bfloat16),
        in_specs=[anyspace, vmem, anyspace, anyspace, vmem, vmem],
        out_specs=vmem,
        scratch_shapes=[
            pltpu.VMEM((rows, outputs), jnp.float32),
            pltpu.VMEM((rows, features), jnp.bfloat16),
            pltpu.VMEM((features, outputs), jnp.bfloat16),
            pltpu.VMEM((planes, inner, cols, width), jnp.bfloat16),
            pltpu.VMEM((planes, inner, outputs // PLANE, cols), jnp.bfloat16),
            pltpu.VMEM((PLANE, rows, width), jnp.bfloat16),
            pltpu.VMEM((PLANE, 8, rows), jnp.int32),
            pltpu.VMEM((PLANE, rank, rows), jnp.float32),
            pltpu.VMEM((PLANE, rank, rows), jnp.float32),
            pltpu.VMEM((PLANE, rank, rows), jnp.bfloat16),
            pltpu.VMEM((PLANE, outputs // PLANE, rows), jnp.bfloat16),
            pltpu.VMEM((PLANE, outputs // PLANE, rows), jnp.bfloat16),
            dma((planes, inner)),
            dma((planes, inner)),
            dma((planes, inner)),
            dma((planes, inner)),
            dma((inner,)),
            dma((planes, inner)),
            dma((planes, inner)),
            dma((inner,)),
            dma((PLANE,)),
            dma((PLANE,)),
            dma((PLANE,)),
            dma((PLANE,)),
            dma((PLANE,)),
            dma((PLANE,)),
            dma((PLANE,)),
            dma((PLANE,)),
            dma((PLANE,)),
            dma((PLANE,)),
            dma((4,)),
        ],
        compiler_params=pltpu.CompilerParams(
            collective_id=0, has_side_effects=True, vmem_limit_bytes=56 * 1024 * 1024
        ),
        cost_estimate=pl.CostEstimate(
            flops=12 * 10**9, bytes_accessed=250 * 10**6, transcendentals=0
        ),
    )(
        residual_rows,
        gain,
        value_base_weight,
        down,
        up,
        jnp.broadcast_to(slot[None, :], (8, rows)),
    )


def solution(mesh):
    return jax.shard_map(
        shards,
        mesh=mesh,
        in_specs=(
            P(("replica", "req"), None),
            P(),
            P(),
            P("req", None, None),
            P("req", None, None),
            P("replica"),
            P(("replica", "req")),
        ),
        out_specs=P(("replica", "req"), None),
        check_vma=False,
    )
```

```python
import functools

import jax
import jax.numpy as jnp
from jax import lax
from jax.experimental import pallas as pl
from jax.experimental.pallas import tpu as pltpu
from jax.sharding import PartitionSpec as P

MESH = pl.DeviceIdType.MESH
PLANE = 8


def kernel(
    replicas,
    inner,
    planes,
    stored,
    rank,
    x_hbm,
    gain_ref,
    base_w_hbm,
    down_hbm,
    up_ref,
    slot_ref,
    out_ref,
    base_ref,
    square,
    hot,
    x_v,
    w_v,
    down_buf,
    up_buf,
    rows_buf,
    slot_buf,
    acc,
    part_buf,
    shrink_buf,
    answer,
    delta_buf,
    down_recv,
    small_recv,
    small_up,
    small_dn,
    small_plane,
    up_send,
    dn_send,
    plane_send,
    rows_send,
    rows_recv,
    slot_send,
    slot_recv,
    part_send,
    part_recv,
    shrink_send,
    shrink_recv,
    delta_send,
    delta_recv,
    local_sem,
):
    r = lax.axis_index("replica")
    q = lax.axis_index("req")
    z = q // inner
    i = q % inner
    e = r * inner + i
    rows = x_hbm.shape[0]
    width = x_hbm.shape[1] // PLANE
    cols = stored * rank

    def peer(k):
        e2 = lax.rem(e + k, PLANE)
        return e2, (e2 // inner, z * inner + lax.rem(e2, inner))

    has_up = z < planes - 1
    has_dn = z > 0
    above = (r, jnp.minimum(z + 1, planes - 1) * inner + i)
    below = (r, jnp.maximum(z - 1, 0) * inner + i)

    own_x = pltpu.make_async_copy(x_hbm, x_v, local_sem.at[0])
    own_w = pltpu.make_async_copy(base_w_hbm, w_v, local_sem.at[1])
    own_down = pltpu.make_async_copy(
        down_hbm.at[:, pl.ds(pl.multiple_of(e * width, width), width)],
        down_buf.at[z, i],
        local_sem.at[2],
    )
    own_down.start()
    own_x.start()

    barrier = pltpu.get_barrier_semaphore()
    for k in range(1, PLANE):
        pl.semaphore_signal(barrier, inc=1, device_id=peer(k)[1], device_id_type=MESH)

    @pl.when(has_up)
    def _():
        pl.semaphore_signal(barrier, inc=1, device_id=above, device_id_type=MESH)

    @pl.when(has_dn)
    def _():
        pl.semaphore_signal(barrier, inc=1, device_id=below, device_id_type=MESH)

    lines = jnp.where(has_up, 1, 0) + jnp.where(has_dn, 1, 0)
    pl.semaphore_wait(barrier, PLANE - 1 + lines)

    def plane_copy(k):
        i2 = lax.rem(i + k, inner)
        e2 = r * inner + i2
        return pltpu.make_async_remote_copy(
            src_ref=down_hbm.at[:, pl.ds(pl.multiple_of(e2 * width, width), width)],
            dst_ref=down_buf.at[z, i],
            send_sem=plane_send.at[k],
            recv_sem=down_recv.at[z, i],
            device_id=(r, z * inner + i2),
            device_id_type=MESH,
        )

    share = up_ref.shape[0] // PLANE

    def small_copy(k):
        i2 = lax.rem(i + k, inner)
        e2 = r * inner + i2
        return pltpu.make_async_remote_copy(
            src_ref=up_ref.at[pl.ds(pl.multiple_of(e2 * share, share), share)],
            dst_ref=up_buf.at[z, i],
            send_sem=small_plane.at[k],
            recv_sem=small_recv.at[z, i],
            device_id=(r, z * inner + i2),
            device_id_type=MESH,
        )

    def small_line(b, j, up):
        return pltpu.make_async_remote_copy(
            src_ref=up_buf.at[b, j],
            dst_ref=up_buf.at[b, j],
            send_sem=(small_up if up else small_dn).at[b, j],
            recv_sem=small_recv.at[b, j],
            device_id=above if up else below,
            device_id_type=MESH,
        )

    def rows_copy(k):
        e2, dev = peer(k)
        return pltpu.make_async_remote_copy(
            src_ref=x_hbm.at[:, pl.ds(pl.multiple_of(e2 * width, width), width)],
            dst_ref=rows_buf.at[e],
            send_sem=rows_send.at[k],
            recv_sem=rows_recv.at[e],
            device_id=dev,
            device_id_type=MESH,
        )

    def slot_copy(k):
        _, dev = peer(k)
        return pltpu.make_async_remote_copy(
            src_ref=slot_ref,
            dst_ref=slot_buf.at[e],
            send_sem=slot_send.at[k],
            recv_sem=slot_recv.at[e],
            device_id=dev,
            device_id_type=MESH,
        )

    def line_copy(b, j, up):
        return pltpu.make_async_remote_copy(
            src_ref=down_buf.at[b, j],
            dst_ref=down_buf.at[b, j],
            send_sem=(up_send if up else dn_send).at[b, j],
            recv_sem=down_recv.at[b, j],
            device_id=above if up else below,
            device_id_type=MESH,
        )

    def block_recv(b, j):
        pltpu.make_async_remote_copy(
            src_ref=down_buf.at[b, j],
            dst_ref=down_buf.at[b, j],
            send_sem=up_send.at[b, j],
            recv_sem=down_recv.at[b, j],
            device_id=above,
            device_id_type=MESH,
        ).wait_recv()
        small_line(b, j, True).wait_recv()

    def pass_on(b, j, up):
        @pl.when(has_up if up else has_dn)
        def _():
            line_copy(b, j, up).start()
            small_line(b, j, up).start()

    for k in range(1, inner):
        plane_copy(k).start()
        small_copy(k).start()
    up_buf[z, i] = up_ref[pl.ds(pl.multiple_of(e * share, share), share), :]
    own_down.wait()
    pass_on(z, i, True)
    pass_on(z, i, False)
    for k in range(1, PLANE):
        slot_copy(k).start()
        if k % inner == 0:
            rows_copy(k).start()
    own_w.start()
    slot_buf[e] = slot_ref[...]
    for k in range(1, inner):
        j = lax.rem(i + k, inner)
        block_recv(z, j)
        pass_on(z, j, True)
        pass_on(z, j, False)

    for k in range(1, PLANE):
        if k % inner:
            rows_copy(k).start()

    own_x.wait()
    own_w.wait()
    base_ref[...] = jnp.zeros_like(base_ref)
    square[...] = jnp.zeros_like(square)

    def base_step(c):
        at = pl.multiple_of(c * width, width)
        wide = x_v[:, pl.ds(at, width)].astype(jnp.float32)
        square[...] += jnp.sum(wide * wide, axis=1, keepdims=True)
        scaled = (wide * gain_ref[c]).astype(jnp.bfloat16)
        x_v[:, pl.ds(at, width)] = scaled
        base_ref[...] += jnp.dot(
            scaled, w_v[pl.ds(at, width), :], preferred_element_type=jnp.float32
        )

    def take(s):
        @pl.when(z - s >= 0)
        def _():
            @pl.loop(0, inner)
            def _(j):
                block_recv(z - s, j)

        @pl.when(z + s < planes)
        def _():
            @pl.loop(0, inner)
            def _(j):
                block_recv(z + s, j)

    gain_own = gain_ref[e]

    def multiply(b):
        down = down_buf[b].reshape(inner * cols, width)

        @pl.loop(0, PLANE)
        def _(n):
            product = lax.dot_general(
                down,
                rows_buf[n],
                (((1,), (1,)), ((), ())),
                preferred_element_type=jnp.float32,
            )
            slots = slot_buf[n][0:1, :]
            total = acc[n]
            for j in range(inner):
                for w in range(stored):
                    at = (j * stored + w) * rank
                    mine = slots == (b * inner + j) * stored + w
                    total = jnp.where(mine, product[at : at + rank], total)
            acc[n] = total

    @pl.loop(0, (planes - 2) * inner)
    def _(t):
        s = t // inner + 1
        j = t % inner

        @pl.when(z - s >= 0)
        def _():
            block_recv(z - s, j)
            pass_on(z - s, j, True)

        @pl.when(z + s < planes)
        def _():
            block_recv(z + s, j)
            pass_on(z + s, j, False)

        @pl.when(t < PLANE)
        def _():
            base_step(t)

    @pl.loop(min((planes - 2) * inner, PLANE), PLANE)
    def _(c):
        base_step(c)

    factor = lax.rsqrt(square[...] / (width * PLANE) + 1e-05)
    base_ref[...] = base_ref[...] * factor[:, 0:1]
    factor_row = jnp.transpose(factor)[0:1, :]

    own_rows = pltpu.make_async_copy(
        x_v.at[:, pl.ds(pl.multiple_of(e * width, width), width)],
        rows_buf.at[e],
        local_sem.at[3],
    )
    own_rows.start()
    acc[...] = jnp.zeros_like(acc)
    own_rows.wait()
    for k in range(1, PLANE):
        e2, dev = peer(k)
        pltpu.make_async_remote_copy(
            src_ref=slot_ref,
            dst_ref=slot_buf.at[e2],
            send_sem=slot_send.at[k],
            recv_sem=slot_recv.at[e2],
            device_id=dev,
            device_id_type=MESH,
        ).wait_recv()
        pltpu.make_async_remote_copy(
            src_ref=rows_buf.at[e2],
            dst_ref=rows_buf.at[e2],
            send_sem=rows_send.at[k],
            recv_sem=rows_recv.at[e2],
            device_id=dev,
            device_id_type=MESH,
        ).wait_recv()
        rows_buf[e2] = (rows_buf[e2].astype(jnp.float32) * gain_own).astype(jnp.bfloat16)

    multiply(z)

    @pl.loop(0, PLANE)
    def _(n):
        slots = jnp.broadcast_to(slot_buf[n][0:1, :], (16, rows))

        @pl.loop(0, planes * inner * stored)
        def _(a):
            hot[n, a] = jnp.where(slots == a, 1.0, 0.0).astype(jnp.bfloat16)

    @pl.loop(1, planes)
    def _(s):
        @pl.when(s == planes - 1)
        def _():
            take(s)

        @pl.when(z - s >= 0)
        def _():
            multiply(z - s)

        @pl.when(z + s < planes)
        def _():
            multiply(z + s)

    def part_copy(k):
        e2, dev = peer(k)
        return pltpu.make_async_remote_copy(
            src_ref=acc.at[e2],
            dst_ref=part_buf.at[e],
            send_sem=part_send.at[k],
            recv_sem=part_recv.at[e],
            device_id=dev,
            device_id_type=MESH,
        )

    for k in range(1, PLANE):
        part_copy(k).start()
    total = acc[e]
    for k in range(1, PLANE):
        e2, dev = peer(k)
        pltpu.make_async_remote_copy(
            src_ref=part_buf.at[e2],
            dst_ref=part_buf.at[e2],
            send_sem=part_send.at[k],
            recv_sem=part_recv.at[e2],
            device_id=dev,
            device_id_type=MESH,
        ).wait_recv()
        total += part_buf[e2]
    shrink_buf[e] = (total * factor_row).astype(jnp.bfloat16)

    def shrink_copy(k):
        _, dev = peer(k)
        return pltpu.make_async_remote_copy(
            src_ref=shrink_buf.at[e],
            dst_ref=shrink_buf.at[e],
            send_sem=shrink_send.at[k],
            recv_sem=shrink_recv.at[e],
            device_id=dev,
            device_id_type=MESH,
        )

    def delta_copy(k):
        e2, dev = peer(k)
        return pltpu.make_async_remote_copy(
            src_ref=answer.at[e2],
            dst_ref=delta_buf.at[e],
            send_sem=delta_send.at[k],
            recv_sem=delta_recv.at[e],
            device_id=dev,
            device_id_type=MESH,
        )

    def expand(n):
        shrunk = shrink_buf[n].reshape(rank // 16, 16, rows)

        def block(b, total):
            spread = jnp.concatenate(
                [
                    (shrunk * hot[n, b * inner * stored + a][None]).reshape(rank, rows)
                    for a in range(inner * stored)
                ],
                axis=0,
            )
            for j in range(inner):
                total += jnp.dot(
                    up_buf[b, j],
                    spread[j * cols : (j + 1) * cols],
                    preferred_element_type=jnp.float32,
                )
            return total

        zero = jnp.zeros((share, rows), jnp.float32)
        return lax.fori_loop(0, planes, block, zero).astype(jnp.bfloat16)

    for k in range(1, PLANE):
        shrink_copy(k).start()
    delta_buf[e] = expand(e)
    for k in range(1, PLANE):
        e2, dev = peer(k)
        pltpu.make_async_remote_copy(
            src_ref=shrink_buf.at[e2],
            dst_ref=shrink_buf.at[e2],
            send_sem=shrink_send.at[k],
            recv_sem=shrink_recv.at[e2],
            device_id=dev,
            device_id_type=MESH,
        ).wait_recv()
        answer[e2] = expand(e2)
        delta_copy(k).start()
    for k in range(1, PLANE):
        e2, dev = peer(k)
        pltpu.make_async_remote_copy(
            src_ref=delta_buf.at[e2],
            dst_ref=delta_buf.at[e2],
            send_sem=delta_send.at[k],
            recv_sem=delta_recv.at[e2],
            device_id=dev,
            device_id_type=MESH,
        ).wait_recv()
    delta = delta_buf[...].reshape(PLANE * share, rows).astype(jnp.float32)
    out_ref[...] = (base_ref[...] + jnp.transpose(delta)).astype(jnp.bfloat16)

    for k in range(1, inner):
        plane_copy(k).wait_send()
        small_copy(k).wait_send()
    for k in range(1, PLANE):
        slot_copy(k).wait_send()
        rows_copy(k).wait_send()
        part_copy(k).wait_send()
        shrink_copy(k).wait_send()
        delta_copy(k).wait_send()

    @pl.loop(0, planes)
    def _(b):
        @pl.when(jnp.logical_and(has_up, b <= z))
        def _():
            @pl.loop(0, inner)
            def _(j):
                line_copy(b, j, True).wait_send()
                small_line(b, j, True).wait_send()

        @pl.when(jnp.logical_and(has_dn, b >= z))
        def _():
            @pl.loop(0, inner)
            def _(j):
                line_copy(b, j, False).wait_send()
                small_line(b, j, False).wait_send()


def shards(
    residual_rows,
    attention_norm_gain,
    value_base_weight,
    adapter_down_weight,
    adapter_up_weight,
    adapter_storage_slot,
    request_adapter_index,
):
    replicas = lax.axis_size("replica")
    devices = lax.axis_size("req")
    inner = PLANE // replicas
    planes = devices // inner
    rows, features = residual_rows.shape
    width = features // PLANE
    stored, _, rank = adapter_down_weight.shape
    outputs = value_base_weight.shape[1]
    cols = stored * rank
    adapter_ids = jnp.arange(adapter_storage_slot.shape[0], dtype=jnp.int32)
    slot_hot = request_adapter_index[:, None] == adapter_ids[None, :]
    slot = jnp.sum(jnp.where(slot_hot, adapter_storage_slot[None, :], 0), axis=1)
    up = jnp.transpose(adapter_up_weight, (2, 0, 1)).reshape(outputs, cols)
    down = jnp.transpose(adapter_down_weight, (0, 2, 1)).reshape(cols, features)
    gain = attention_norm_gain.astype(jnp.float32).reshape(PLANE, 1, width)
    anyspace = pl.BlockSpec(memory_space=pl.ANY)
    vmem = pl.BlockSpec(memory_space=pltpu.VMEM)
    dma = pltpu.SemaphoreType.DMA
    return pl.pallas_call(
        functools.partial(kernel, replicas, inner, planes, stored, rank),
        out_shape=jax.ShapeDtypeStruct((rows, outputs), jnp.bfloat16),
        in_specs=[anyspace, vmem, anyspace, anyspace, vmem, vmem],
        out_specs=vmem,
        scratch_shapes=[
            pltpu.VMEM((rows, outputs), jnp.float32),
            pltpu.VMEM((rows, 128), jnp.float32),
            pltpu.VMEM((PLANE, adapter_ids.shape[0], 16, rows), jnp.bfloat16),
            pltpu.VMEM((rows, features), jnp.bfloat16),
            pltpu.VMEM((features, outputs), jnp.bfloat16),
            pltpu.VMEM((planes, inner, cols, width), jnp.bfloat16),
            pltpu.VMEM((planes, inner, outputs // PLANE, cols), jnp.bfloat16),
            pltpu.VMEM((PLANE, rows, width), jnp.bfloat16),
            pltpu.VMEM((PLANE, 8, rows), jnp.int32),
            pltpu.VMEM((PLANE, rank, rows), jnp.float32),
            pltpu.VMEM((PLANE, rank, rows), jnp.float32),
            pltpu.VMEM((PLANE, rank, rows), jnp.bfloat16),
            pltpu.VMEM((PLANE, outputs // PLANE, rows), jnp.bfloat16),
            pltpu.VMEM((PLANE, outputs // PLANE, rows), jnp.bfloat16),
            dma((planes, inner)),
            dma((planes, inner)),
            dma((planes, inner)),
            dma((planes, inner)),
            dma((inner,)),
            dma((planes, inner)),
            dma((planes, inner)),
            dma((inner,)),
            dma((PLANE,)),
            dma((PLANE,)),
            dma((PLANE,)),
            dma((PLANE,)),
            dma((PLANE,)),
            dma((PLANE,)),
            dma((PLANE,)),
            dma((PLANE,)),
            dma((PLANE,)),
            dma((PLANE,)),
            dma((4,)),
        ],
        compiler_params=pltpu.CompilerParams(
            collective_id=0, has_side_effects=True, vmem_limit_bytes=56 * 1024 * 1024
        ),
        cost_estimate=pl.CostEstimate(
            flops=12 * 10**9, bytes_accessed=250 * 10**6, transcendentals=0
        ),
    )(
        residual_rows,
        gain,
        value_base_weight,
        down,
        up,
        jnp.broadcast_to(slot[None, :], (8, rows)),
    )


def solution(mesh):
    return jax.shard_map(
        shards,
        mesh=mesh,
        in_specs=(
            P(("replica", "req"), None),
            P(),
            P(),
            P("req", None, None),
            P("req", None, None),
            P("replica"),
            P(("replica", "req")),
        ),
        out_specs=P(("replica", "req"), None),
        check_vma=False,
    )
```

```python
import functools

import jax
import jax.numpy as jnp
from jax import lax
from jax.experimental import pallas as pl
from jax.experimental.pallas import tpu as pltpu
from jax.sharding import PartitionSpec as P

MESH = pl.DeviceIdType.MESH
PLANE = 8


def kernel(
    replicas,
    inner,
    planes,
    stored,
    rank,
    x_hbm,
    gain_ref,
    base_w_hbm,
    down_hbm,
    up_ref,
    slot_ref,
    out_ref,
    base_ref,
    square,
    hot,
    x_v,
    w_v,
    down_buf,
    up_buf,
    rows_buf,
    slot_buf,
    acc,
    part_buf,
    shrink_buf,
    answer,
    delta_buf,
    down_recv,
    small_recv,
    small_up,
    small_dn,
    small_plane,
    up_send,
    dn_send,
    plane_send,
    rows_send,
    rows_recv,
    slot_send,
    slot_recv,
    part_send,
    part_recv,
    shrink_send,
    shrink_recv,
    delta_send,
    delta_recv,
    local_sem,
):
    r = lax.axis_index("replica")
    q = lax.axis_index("req")
    z = q // inner
    i = q % inner
    e = r * inner + i
    rows = x_hbm.shape[0]
    width = x_hbm.shape[1] // PLANE
    cols = stored * rank

    def peer(k):
        e2 = 0
        for bit in (1, 2, 4):
            own = (e // bit) % 2
            e2 += bit * (1 - own if k & bit else own)
        return e2, (e2 // inner, z * inner + lax.rem(e2, inner))

    has_up = z < planes - 1
    has_dn = z > 0
    above = (r, jnp.minimum(z + 1, planes - 1) * inner + i)
    below = (r, jnp.maximum(z - 1, 0) * inner + i)

    own_x = pltpu.make_async_copy(x_hbm, x_v, local_sem.at[0])
    own_w = pltpu.make_async_copy(base_w_hbm, w_v, local_sem.at[1])
    own_down = pltpu.make_async_copy(
        down_hbm.at[:, pl.ds(pl.multiple_of(e * width, width), width)],
        down_buf.at[z, i],
        local_sem.at[2],
    )
    own_down.start()
    own_x.start()

    barrier = pltpu.get_barrier_semaphore()
    for k in range(1, PLANE):
        pl.semaphore_signal(barrier, inc=1, device_id=peer(k)[1], device_id_type=MESH)

    @pl.when(has_up)
    def _():
        pl.semaphore_signal(barrier, inc=1, device_id=above, device_id_type=MESH)

    @pl.when(has_dn)
    def _():
        pl.semaphore_signal(barrier, inc=1, device_id=below, device_id_type=MESH)

    lines = jnp.where(has_up, 1, 0) + jnp.where(has_dn, 1, 0)
    pl.semaphore_wait(barrier, PLANE - 1 + lines)

    def plane_copy(k):
        i2 = lax.rem(i + k, inner)
        e2 = r * inner + i2
        return pltpu.make_async_remote_copy(
            src_ref=down_hbm.at[:, pl.ds(pl.multiple_of(e2 * width, width), width)],
            dst_ref=down_buf.at[z, i],
            send_sem=plane_send.at[k],
            recv_sem=down_recv.at[z, i],
            device_id=(r, z * inner + i2),
            device_id_type=MESH,
        )

    share = up_ref.shape[0] // PLANE

    def small_copy(k):
        i2 = lax.rem(i + k, inner)
        e2 = r * inner + i2
        return pltpu.make_async_remote_copy(
            src_ref=up_ref.at[pl.ds(pl.multiple_of(e2 * share, share), share)],
            dst_ref=up_buf.at[z, i],
            send_sem=small_plane.at[k],
            recv_sem=small_recv.at[z, i],
            device_id=(r, z * inner + i2),
            device_id_type=MESH,
        )

    def small_line(b, j, up):
        return pltpu.make_async_remote_copy(
            src_ref=up_buf.at[b, j],
            dst_ref=up_buf.at[b, j],
            send_sem=(small_up if up else small_dn).at[b, j],
            recv_sem=small_recv.at[b, j],
            device_id=above if up else below,
            device_id_type=MESH,
        )

    def rows_copy(k):
        e2, dev = peer(k)
        return pltpu.make_async_remote_copy(
            src_ref=x_hbm.at[:, pl.ds(pl.multiple_of(e2 * width, width), width)],
            dst_ref=rows_buf.at[e],
            send_sem=rows_send.at[k],
            recv_sem=rows_recv.at[e],
            device_id=dev,
            device_id_type=MESH,
        )

    def slot_copy(k):
        _, dev = peer(k)
        return pltpu.make_async_remote_copy(
            src_ref=slot_ref,
            dst_ref=slot_buf.at[e],
            send_sem=slot_send.at[k],
            recv_sem=slot_recv.at[e],
            device_id=dev,
            device_id_type=MESH,
        )

    def line_copy(b, j, up):
        return pltpu.make_async_remote_copy(
            src_ref=down_buf.at[b, j],
            dst_ref=down_buf.at[b, j],
            send_sem=(up_send if up else dn_send).at[b, j],
            recv_sem=down_recv.at[b, j],
            device_id=above if up else below,
            device_id_type=MESH,
        )

    def block_recv(b, j):
        pltpu.make_async_remote_copy(
            src_ref=down_buf.at[b, j],
            dst_ref=down_buf.at[b, j],
            send_sem=up_send.at[b, j],
            recv_sem=down_recv.at[b, j],
            device_id=above,
            device_id_type=MESH,
        ).wait_recv()
        small_line(b, j, True).wait_recv()

    def pass_on(b, j, up):
        @pl.when(has_up if up else has_dn)
        def _():
            line_copy(b, j, up).start()
            small_line(b, j, up).start()

    for k in range(1, inner):
        plane_copy(k).start()
        small_copy(k).start()
    up_buf[z, i] = up_ref[pl.ds(pl.multiple_of(e * share, share), share), :]
    own_down.wait()
    pass_on(z, i, True)
    pass_on(z, i, False)
    for k in range(1, PLANE):
        slot_copy(k).start()
        if not k & 2:
            rows_copy(k).start()
    own_w.start()
    slot_buf[e] = slot_ref[...]
    for k in range(1, inner):
        j = lax.rem(i + k, inner)
        block_recv(z, j)
        pass_on(z, j, True)
        pass_on(z, j, False)

    for k in range(1, PLANE):
        if k & 2:
            rows_copy(k).start()

    own_x.wait()
    own_w.wait()
    base_ref[...] = jnp.zeros_like(base_ref)
    square[...] = jnp.zeros_like(square)

    def base_step(c):
        at = pl.multiple_of(c * width, width)
        wide = x_v[:, pl.ds(at, width)].astype(jnp.float32)
        square[...] += jnp.sum(wide * wide, axis=1, keepdims=True)
        scaled = (wide * gain_ref[c]).astype(jnp.bfloat16)
        x_v[:, pl.ds(at, width)] = scaled
        base_ref[...] += jnp.dot(
            scaled, w_v[pl.ds(at, width), :], preferred_element_type=jnp.float32
        )

    gain_own = gain_ref[e]

    def multiply(n, down, first):
        product = lax.dot_general(
            down,
            rows_buf[n],
            (((1,), (1,)), ((), ())),
            preferred_element_type=jnp.float32,
        )
        slots = slot_buf[n][0:1, :]
        total = acc[n]
        for a in range(down.shape[0] // rank):
            total = jnp.where(slots == first + a, product[a * rank : (a + 1) * rank], total)
        acc[n] = total

    def multiply_row(n):
        @pl.loop(0, planes)
        def _(b):
            far = jnp.maximum(b - z, z - b)

            @pl.when(far < planes - 1)
            def _():
                multiply(n, down_buf[b].reshape(inner * cols, width), b * inner * stored)

    def multiply_last(b):
        @pl.loop(0, inner)
        def _(j):
            block_recv(b, j)

            @pl.loop(0, PLANE)
            def _(n):
                multiply(n, down_buf[b, j], (b * inner + j) * stored)

    @pl.loop(0, (planes - 2) * inner)
    def _(t):
        s = t // inner + 1
        j = t % inner

        @pl.when(z - s >= 0)
        def _():
            block_recv(z - s, j)
            pass_on(z - s, j, True)

        @pl.when(z + s < planes)
        def _():
            block_recv(z + s, j)
            pass_on(z + s, j, False)

        @pl.when(t < PLANE)
        def _():
            base_step(t)

    @pl.loop(min((planes - 2) * inner, PLANE), PLANE)
    def _(c):
        base_step(c)

    factor = lax.rsqrt(square[...] / (width * PLANE) + 1e-05)
    base_ref[...] = base_ref[...] * factor[:, 0:1]
    factor_row = jnp.transpose(factor)[0:1, :]

    own_rows = pltpu.make_async_copy(
        x_v.at[:, pl.ds(pl.multiple_of(e * width, width), width)],
        rows_buf.at[e],
        local_sem.at[3],
    )
    own_rows.start()
    acc[...] = jnp.zeros_like(acc)
    for k in range(1, PLANE):
        e2, dev = peer(k)
        pltpu.make_async_remote_copy(
            src_ref=slot_ref,
            dst_ref=slot_buf.at[e2],
            send_sem=slot_send.at[k],
            recv_sem=slot_recv.at[e2],
            device_id=dev,
            device_id_type=MESH,
        ).wait_recv()

    @pl.loop(0, PLANE)
    def _(n):
        slots = jnp.broadcast_to(slot_buf[n][0:1, :], (16, rows))

        @pl.loop(0, planes * inner * stored)
        def _(a):
            hot[n, a] = jnp.where(slots == a, 1.0, 0.0).astype(jnp.bfloat16)

    own_rows.wait()
    multiply_row(e)
    for k in (1, 4, 5, 2, 3, 6, 7):
        e2, dev = peer(k)
        pltpu.make_async_remote_copy(
            src_ref=rows_buf.at[e2],
            dst_ref=rows_buf.at[e2],
            send_sem=rows_send.at[k],
            recv_sem=rows_recv.at[e2],
            device_id=dev,
            device_id_type=MESH,
        ).wait_recv()
        rows_buf[e2] = (rows_buf[e2].astype(jnp.float32) * gain_own).astype(jnp.bfloat16)
        multiply_row(e2)

    @pl.when(z == 0)
    def _():
        multiply_last(planes - 1)

    @pl.when(z == planes - 1)
    def _():
        multiply_last(0)

    def part_copy(k):
        e2, dev = peer(k)
        return pltpu.make_async_remote_copy(
            src_ref=acc.at[e2],
            dst_ref=part_buf.at[e],
            send_sem=part_send.at[k],
            recv_sem=part_recv.at[e],
            device_id=dev,
            device_id_type=MESH,
        )

    for k in range(1, PLANE):
        part_copy(k).start()
    total = acc[e]
    for k in range(1, PLANE):
        e2, dev = peer(k)
        pltpu.make_async_remote_copy(
            src_ref=part_buf.at[e2],
            dst_ref=part_buf.at[e2],
            send_sem=part_send.at[k],
            recv_sem=part_recv.at[e2],
            device_id=dev,
            device_id_type=MESH,
        ).wait_recv()
        total += part_buf[e2]
    shrink_buf[e] = (total * factor_row).astype(jnp.bfloat16)

    def shrink_copy(k):
        _, dev = peer(k)
        return pltpu.make_async_remote_copy(
            src_ref=shrink_buf.at[e],
            dst_ref=shrink_buf.at[e],
            send_sem=shrink_send.at[k],
            recv_sem=shrink_recv.at[e],
            device_id=dev,
            device_id_type=MESH,
        )

    def delta_copy(k):
        e2, dev = peer(k)
        return pltpu.make_async_remote_copy(
            src_ref=answer.at[e2],
            dst_ref=delta_buf.at[e],
            send_sem=delta_send.at[k],
            recv_sem=delta_recv.at[e],
            device_id=dev,
            device_id_type=MESH,
        )

    def expand(n):
        shrunk = shrink_buf[n].reshape(rank // 16, 16, rows)

        def block(b, total):
            spread = jnp.concatenate(
                [
                    (shrunk * hot[n, b * inner * stored + a][None]).reshape(rank, rows)
                    for a in range(inner * stored)
                ],
                axis=0,
            )
            for j in range(inner):
                total += jnp.dot(
                    up_buf[b, j],
                    spread[j * cols : (j + 1) * cols],
                    preferred_element_type=jnp.float32,
                )
            return total

        zero = jnp.zeros((share, rows), jnp.float32)
        return lax.fori_loop(0, planes, block, zero).astype(jnp.bfloat16)

    for k in range(1, PLANE):
        shrink_copy(k).start()
    delta_buf[e] = expand(e)
    for k in range(1, PLANE):
        e2, dev = peer(k)
        pltpu.make_async_remote_copy(
            src_ref=shrink_buf.at[e2],
            dst_ref=shrink_buf.at[e2],
            send_sem=shrink_send.at[k],
            recv_sem=shrink_recv.at[e2],
            device_id=dev,
            device_id_type=MESH,
        ).wait_recv()
        answer[e2] = expand(e2)
        delta_copy(k).start()
    for k in range(1, PLANE):
        e2, dev = peer(k)
        pltpu.make_async_remote_copy(
            src_ref=delta_buf.at[e2],
            dst_ref=delta_buf.at[e2],
            send_sem=delta_send.at[k],
            recv_sem=delta_recv.at[e2],
            device_id=dev,
            device_id_type=MESH,
        ).wait_recv()
    delta = delta_buf[...].reshape(PLANE * share, rows).astype(jnp.float32)
    out_ref[...] = (base_ref[...] + jnp.transpose(delta)).astype(jnp.bfloat16)

    for k in range(1, inner):
        plane_copy(k).wait_send()
        small_copy(k).wait_send()
    for k in range(1, PLANE):
        slot_copy(k).wait_send()
        rows_copy(k).wait_send()
        part_copy(k).wait_send()
        shrink_copy(k).wait_send()
        delta_copy(k).wait_send()

    @pl.loop(0, planes)
    def _(b):
        @pl.when(jnp.logical_and(has_up, b <= z))
        def _():
            @pl.loop(0, inner)
            def _(j):
                line_copy(b, j, True).wait_send()
                small_line(b, j, True).wait_send()

        @pl.when(jnp.logical_and(has_dn, b >= z))
        def _():
            @pl.loop(0, inner)
            def _(j):
                line_copy(b, j, False).wait_send()
                small_line(b, j, False).wait_send()


def shards(
    residual_rows,
    attention_norm_gain,
    value_base_weight,
    adapter_down_weight,
    adapter_up_weight,
    adapter_storage_slot,
    request_adapter_index,
):
    replicas = lax.axis_size("replica")
    devices = lax.axis_size("req")
    inner = PLANE // replicas
    planes = devices // inner
    rows, features = residual_rows.shape
    width = features // PLANE
    stored, _, rank = adapter_down_weight.shape
    outputs = value_base_weight.shape[1]
    cols = stored * rank
    adapter_ids = jnp.arange(adapter_storage_slot.shape[0], dtype=jnp.int32)
    slot_hot = request_adapter_index[:, None] == adapter_ids[None, :]
    slot = jnp.sum(jnp.where(slot_hot, adapter_storage_slot[None, :], 0), axis=1)
    up = jnp.transpose(adapter_up_weight, (2, 0, 1)).reshape(outputs, cols)
    down = jnp.transpose(adapter_down_weight, (0, 2, 1)).reshape(cols, features)
    gain = attention_norm_gain.astype(jnp.float32).reshape(PLANE, 1, width)
    anyspace = pl.BlockSpec(memory_space=pl.ANY)
    vmem = pl.BlockSpec(memory_space=pltpu.VMEM)
    dma = pltpu.SemaphoreType.DMA
    return pl.pallas_call(
        functools.partial(kernel, replicas, inner, planes, stored, rank),
        out_shape=jax.ShapeDtypeStruct((rows, outputs), jnp.bfloat16),
        in_specs=[anyspace, vmem, anyspace, anyspace, vmem, vmem],
        out_specs=vmem,
        scratch_shapes=[
            pltpu.VMEM((rows, outputs), jnp.float32),
            pltpu.VMEM((rows, 128), jnp.float32),
            pltpu.VMEM((PLANE, adapter_ids.shape[0], 16, rows), jnp.bfloat16),
            pltpu.VMEM((rows, features), jnp.bfloat16),
            pltpu.VMEM((features, outputs), jnp.bfloat16),
            pltpu.VMEM((planes, inner, cols, width), jnp.bfloat16),
            pltpu.VMEM((planes, inner, outputs // PLANE, cols), jnp.bfloat16),
            pltpu.VMEM((PLANE, rows, width), jnp.bfloat16),
            pltpu.VMEM((PLANE, 8, rows), jnp.int32),
            pltpu.VMEM((PLANE, rank, rows), jnp.float32),
            pltpu.VMEM((PLANE, rank, rows), jnp.float32),
            pltpu.VMEM((PLANE, rank, rows), jnp.bfloat16),
            pltpu.VMEM((PLANE, outputs // PLANE, rows), jnp.bfloat16),
            pltpu.VMEM((PLANE, outputs // PLANE, rows), jnp.bfloat16),
            dma((planes, inner)),
            dma((planes, inner)),
            dma((planes, inner)),
            dma((planes, inner)),
            dma((inner,)),
            dma((planes, inner)),
            dma((planes, inner)),
            dma((inner,)),
            dma((PLANE,)),
            dma((PLANE,)),
            dma((PLANE,)),
            dma((PLANE,)),
            dma((PLANE,)),
            dma((PLANE,)),
            dma((PLANE,)),
            dma((PLANE,)),
            dma((PLANE,)),
            dma((PLANE,)),
            dma((4,)),
        ],
        compiler_params=pltpu.CompilerParams(
            collective_id=0, has_side_effects=True, vmem_limit_bytes=56 * 1024 * 1024
        ),
        cost_estimate=pl.CostEstimate(
            flops=12 * 10**9, bytes_accessed=250 * 10**6, transcendentals=0
        ),
    )(
        residual_rows,
        gain,
        value_base_weight,
        down,
        up,
        jnp.broadcast_to(slot[None, :], (8, rows)),
    )


def solution(mesh):
    return jax.shard_map(
        shards,
        mesh=mesh,
        in_specs=(
            P(("replica", "req"), None),
            P(),
            P(),
            P("req", None, None),
            P("req", None, None),
            P("replica"),
            P(("replica", "req")),
        ),
        out_specs=P(("replica", "req"), None),
        check_vma=False,
    )
```

```python
import functools

import jax
import jax.numpy as jnp
from jax import lax
from jax.experimental import pallas as pl
from jax.experimental.pallas import tpu as pltpu
from jax.sharding import PartitionSpec as P

MESH = pl.DeviceIdType.MESH
PLANE = 8


def kernel(
    replicas,
    inner,
    planes,
    stored,
    rank,
    x_hbm,
    gain_ref,
    base_w_hbm,
    down_hbm,
    up_ref,
    slot_ref,
    out_ref,
    base_ref,
    square,
    hot,
    x_v,
    w_v,
    down_buf,
    up_buf,
    rows_buf,
    slot_buf,
    acc,
    part_buf,
    shrink_buf,
    answer,
    delta_buf,
    down_recv,
    small_recv,
    small_up,
    small_dn,
    small_plane,
    up_send,
    dn_send,
    plane_send,
    rows_send,
    rows_recv,
    slot_send,
    slot_recv,
    part_send,
    part_recv,
    shrink_send,
    shrink_recv,
    delta_send,
    delta_recv,
    local_sem,
):
    r = lax.axis_index("replica")
    q = lax.axis_index("req")
    z = q // inner
    i = q % inner
    e = r * inner + i
    rows = x_hbm.shape[0]
    width = x_hbm.shape[1] // PLANE
    cols = stored * rank

    def peer(k):
        e2 = 0
        for bit in (1, 2, 4):
            own = (e // bit) % 2
            e2 += bit * (1 - own if k & bit else own)
        return e2, (e2 // inner, z * inner + lax.rem(e2, inner))

    has_up = z < planes - 1
    has_dn = z > 0
    above = (r, jnp.minimum(z + 1, planes - 1) * inner + i)
    below = (r, jnp.maximum(z - 1, 0) * inner + i)

    own_x = pltpu.make_async_copy(x_hbm, x_v, local_sem.at[0])
    own_w = pltpu.make_async_copy(base_w_hbm, w_v, local_sem.at[1])
    own_down = pltpu.make_async_copy(
        down_hbm.at[:, pl.ds(pl.multiple_of(e * width, width), width)],
        down_buf.at[z, i],
        local_sem.at[2],
    )
    own_down.start()
    own_x.start()

    barrier = pltpu.get_barrier_semaphore()
    for k in range(1, PLANE):
        pl.semaphore_signal(barrier, inc=1, device_id=peer(k)[1], device_id_type=MESH)

    @pl.when(has_up)
    def _():
        pl.semaphore_signal(barrier, inc=1, device_id=above, device_id_type=MESH)

    @pl.when(has_dn)
    def _():
        pl.semaphore_signal(barrier, inc=1, device_id=below, device_id_type=MESH)

    lines = jnp.where(has_up, 1, 0) + jnp.where(has_dn, 1, 0)
    pl.semaphore_wait(barrier, PLANE - 1 + lines)

    def plane_copy(k):
        i2 = lax.rem(i + k, inner)
        e2 = r * inner + i2
        return pltpu.make_async_remote_copy(
            src_ref=down_hbm.at[:, pl.ds(pl.multiple_of(e2 * width, width), width)],
            dst_ref=down_buf.at[z, i],
            send_sem=plane_send.at[k],
            recv_sem=down_recv.at[z, i],
            device_id=(r, z * inner + i2),
            device_id_type=MESH,
        )

    share = up_ref.shape[0] // PLANE

    def small_copy(k):
        i2 = lax.rem(i + k, inner)
        e2 = r * inner + i2
        return pltpu.make_async_remote_copy(
            src_ref=up_ref.at[pl.ds(pl.multiple_of(e2 * share, share), share)],
            dst_ref=up_buf.at[z, i],
            send_sem=small_plane.at[k],
            recv_sem=small_recv.at[z, i],
            device_id=(r, z * inner + i2),
            device_id_type=MESH,
        )

    def small_line(b, j, up):
        return pltpu.make_async_remote_copy(
            src_ref=up_buf.at[b, j],
            dst_ref=up_buf.at[b, j],
            send_sem=(small_up if up else small_dn).at[b, j],
            recv_sem=small_recv.at[b, j],
            device_id=above if up else below,
            device_id_type=MESH,
        )

    def rows_copy(k):
        e2, dev = peer(k)
        return pltpu.make_async_remote_copy(
            src_ref=x_hbm.at[:, pl.ds(pl.multiple_of(e2 * width, width), width)],
            dst_ref=rows_buf.at[e],
            send_sem=rows_send.at[k],
            recv_sem=rows_recv.at[e],
            device_id=dev,
            device_id_type=MESH,
        )

    def slot_copy(k):
        _, dev = peer(k)
        return pltpu.make_async_remote_copy(
            src_ref=slot_ref,
            dst_ref=slot_buf.at[e],
            send_sem=slot_send.at[k],
            recv_sem=slot_recv.at[e],
            device_id=dev,
            device_id_type=MESH,
        )

    def line_copy(b, j, up):
        return pltpu.make_async_remote_copy(
            src_ref=down_buf.at[b, j],
            dst_ref=down_buf.at[b, j],
            send_sem=(up_send if up else dn_send).at[b, j],
            recv_sem=down_recv.at[b, j],
            device_id=above if up else below,
            device_id_type=MESH,
        )

    def block_recv(b, j):
        pltpu.make_async_remote_copy(
            src_ref=down_buf.at[b, j],
            dst_ref=down_buf.at[b, j],
            send_sem=up_send.at[b, j],
            recv_sem=down_recv.at[b, j],
            device_id=above,
            device_id_type=MESH,
        ).wait_recv()
        small_line(b, j, True).wait_recv()

    def pass_on(b, j, up):
        @pl.when(has_up if up else has_dn)
        def _():
            line_copy(b, j, up).start()
            small_line(b, j, up).start()

    for k in range(1, inner):
        plane_copy(k).start()
        small_copy(k).start()
    up_buf[z, i] = up_ref[pl.ds(pl.multiple_of(e * share, share), share), :]
    own_down.wait()
    pass_on(z, i, True)
    pass_on(z, i, False)
    for k in range(1, PLANE):
        slot_copy(k).start()
    own_w.start()
    slot_buf[e] = slot_ref[...]
    for k in range(1, inner):
        j = lax.rem(i + k, inner)
        block_recv(z, j)
        pass_on(z, j, True)
        pass_on(z, j, False)

    for k in (1, 4, 5, 2, 3, 6, 7):
        rows_copy(k).start()

    own_x.wait()
    own_w.wait()
    base_ref[...] = jnp.zeros_like(base_ref)
    square[...] = jnp.zeros_like(square)

    def base_step(c):
        at = pl.multiple_of(c * width, width)
        wide = x_v[:, pl.ds(at, width)].astype(jnp.float32)
        square[...] += jnp.sum(wide * wide, axis=1, keepdims=True)
        scaled = (wide * gain_ref[c]).astype(jnp.bfloat16)
        x_v[:, pl.ds(at, width)] = scaled
        base_ref[...] += jnp.dot(
            scaled, w_v[pl.ds(at, width), :], preferred_element_type=jnp.float32
        )

    gain_own = gain_ref[e]

    def multiply(n, down, first):
        product = lax.dot_general(
            down,
            rows_buf[n],
            (((1,), (1,)), ((), ())),
            preferred_element_type=jnp.float32,
        )
        slots = slot_buf[n][0:1, :]
        total = acc[n]
        for a in range(down.shape[0] // rank):
            total = jnp.where(slots == first + a, product[a * rank : (a + 1) * rank], total)
        acc[n] = total

    def multiply_row(n):
        @pl.loop(0, planes)
        def _(b):
            far = jnp.maximum(b - z, z - b)

            @pl.when(far < planes - 1)
            def _():
                multiply(n, down_buf[b].reshape(inner * cols, width), b * inner * stored)

    def multiply_last(b):
        @pl.loop(0, inner)
        def _(j):
            block_recv(b, j)

        @pl.loop(0, PLANE)
        def _(n):
            multiply(n, down_buf[b].reshape(inner * cols, width), b * inner * stored)

    @pl.loop(0, (planes - 2) * inner)
    def _(t):
        s = t // inner + 1
        j = t % inner

        @pl.when(z - s >= 0)
        def _():
            block_recv(z - s, j)
            pass_on(z - s, j, True)

        @pl.when(z + s < planes)
        def _():
            block_recv(z + s, j)
            pass_on(z + s, j, False)

        @pl.when(t < PLANE)
        def _():
            base_step(t)

    @pl.loop(min((planes - 2) * inner, PLANE), PLANE)
    def _(c):
        base_step(c)

    factor = lax.rsqrt(square[...] / (width * PLANE) + 1e-05)
    base_ref[...] = base_ref[...] * factor[:, 0:1]
    factor_row = jnp.transpose(factor)[0:1, :]

    own_rows = pltpu.make_async_copy(
        x_v.at[:, pl.ds(pl.multiple_of(e * width, width), width)],
        rows_buf.at[e],
        local_sem.at[3],
    )
    own_rows.start()
    acc[...] = jnp.zeros_like(acc)
    for k in range(1, PLANE):
        e2, dev = peer(k)
        pltpu.make_async_remote_copy(
            src_ref=slot_ref,
            dst_ref=slot_buf.at[e2],
            send_sem=slot_send.at[k],
            recv_sem=slot_recv.at[e2],
            device_id=dev,
            device_id_type=MESH,
        ).wait_recv()

    @pl.loop(0, PLANE)
    def _(n):
        slots = jnp.broadcast_to(slot_buf[n][0:1, :], (16, rows))

        @pl.loop(0, planes * inner * stored)
        def _(a):
            hot[n, a] = jnp.where(slots == a, 1.0, 0.0).astype(jnp.bfloat16)

    own_rows.wait()
    multiply_row(e)
    for k in (1, 4, 5, 2, 3, 6, 7):
        e2, dev = peer(k)
        pltpu.make_async_remote_copy(
            src_ref=rows_buf.at[e2],
            dst_ref=rows_buf.at[e2],
            send_sem=rows_send.at[k],
            recv_sem=rows_recv.at[e2],
            device_id=dev,
            device_id_type=MESH,
        ).wait_recv()
        rows_buf[e2] = (rows_buf[e2].astype(jnp.float32) * gain_own).astype(jnp.bfloat16)
        multiply_row(e2)

    @pl.when(z == 0)
    def _():
        multiply_last(planes - 1)

    @pl.when(z == planes - 1)
    def _():
        multiply_last(0)

    def part_copy(k):
        e2, dev = peer(k)
        return pltpu.make_async_remote_copy(
            src_ref=acc.at[e2],
            dst_ref=part_buf.at[e],
            send_sem=part_send.at[k],
            recv_sem=part_recv.at[e],
            device_id=dev,
            device_id_type=MESH,
        )

    for k in range(1, PLANE):
        part_copy(k).start()
    total = acc[e]
    for k in range(1, PLANE):
        e2, dev = peer(k)
        pltpu.make_async_remote_copy(
            src_ref=part_buf.at[e2],
            dst_ref=part_buf.at[e2],
            send_sem=part_send.at[k],
            recv_sem=part_recv.at[e2],
            device_id=dev,
            device_id_type=MESH,
        ).wait_recv()
        total += part_buf[e2]
    shrink_buf[e] = (total * factor_row).astype(jnp.bfloat16)

    def shrink_copy(k):
        _, dev = peer(k)
        return pltpu.make_async_remote_copy(
            src_ref=shrink_buf.at[e],
            dst_ref=shrink_buf.at[e],
            send_sem=shrink_send.at[k],
            recv_sem=shrink_recv.at[e],
            device_id=dev,
            device_id_type=MESH,
        )

    def delta_copy(k):
        e2, dev = peer(k)
        return pltpu.make_async_remote_copy(
            src_ref=answer.at[e2],
            dst_ref=delta_buf.at[e],
            send_sem=delta_send.at[k],
            recv_sem=delta_recv.at[e],
            device_id=dev,
            device_id_type=MESH,
        )

    def expand(n):
        shrunk = shrink_buf[n].reshape(rank // 16, 16, rows)

        def block(b, total):
            spread = jnp.concatenate(
                [
                    (shrunk * hot[n, b * inner * stored + a][None]).reshape(rank, rows)
                    for a in range(inner * stored)
                ],
                axis=0,
            )
            for j in range(inner):
                total += jnp.dot(
                    up_buf[b, j],
                    spread[j * cols : (j + 1) * cols],
                    preferred_element_type=jnp.float32,
                )
            return total

        zero = jnp.zeros((share, rows), jnp.float32)
        return lax.fori_loop(0, planes, block, zero).astype(jnp.bfloat16)

    for k in range(1, PLANE):
        shrink_copy(k).start()
    delta_buf[e] = expand(e)
    for k in range(1, PLANE):
        e2, dev = peer(k)
        pltpu.make_async_remote_copy(
            src_ref=shrink_buf.at[e2],
            dst_ref=shrink_buf.at[e2],
            send_sem=shrink_send.at[k],
            recv_sem=shrink_recv.at[e2],
            device_id=dev,
            device_id_type=MESH,
        ).wait_recv()
        answer[e2] = expand(e2)
        delta_copy(k).start()
    for k in range(1, PLANE):
        e2, dev = peer(k)
        pltpu.make_async_remote_copy(
            src_ref=delta_buf.at[e2],
            dst_ref=delta_buf.at[e2],
            send_sem=delta_send.at[k],
            recv_sem=delta_recv.at[e2],
            device_id=dev,
            device_id_type=MESH,
        ).wait_recv()
    delta = delta_buf[...].reshape(PLANE * share, rows).astype(jnp.float32)
    out_ref[...] = (base_ref[...] + jnp.transpose(delta)).astype(jnp.bfloat16)

    for k in range(1, inner):
        plane_copy(k).wait_send()
        small_copy(k).wait_send()
    for k in range(1, PLANE):
        slot_copy(k).wait_send()
        rows_copy(k).wait_send()
        part_copy(k).wait_send()
        shrink_copy(k).wait_send()
        delta_copy(k).wait_send()

    @pl.loop(0, planes)
    def _(b):
        @pl.when(jnp.logical_and(has_up, b <= z))
        def _():
            @pl.loop(0, inner)
            def _(j):
                line_copy(b, j, True).wait_send()
                small_line(b, j, True).wait_send()

        @pl.when(jnp.logical_and(has_dn, b >= z))
        def _():
            @pl.loop(0, inner)
            def _(j):
                line_copy(b, j, False).wait_send()
                small_line(b, j, False).wait_send()


def shards(
    residual_rows,
    attention_norm_gain,
    value_base_weight,
    adapter_down_weight,
    adapter_up_weight,
    adapter_storage_slot,
    request_adapter_index,
):
    replicas = lax.axis_size("replica")
    devices = lax.axis_size("req")
    inner = PLANE // replicas
    planes = devices // inner
    rows, features = residual_rows.shape
    width = features // PLANE
    stored, _, rank = adapter_down_weight.shape
    outputs = value_base_weight.shape[1]
    cols = stored * rank
    adapter_ids = jnp.arange(adapter_storage_slot.shape[0], dtype=jnp.int32)
    slot_hot = request_adapter_index[:, None] == adapter_ids[None, :]
    slot = jnp.sum(jnp.where(slot_hot, adapter_storage_slot[None, :], 0), axis=1)
    up = jnp.transpose(adapter_up_weight, (2, 0, 1)).reshape(outputs, cols)
    down = jnp.transpose(adapter_down_weight, (0, 2, 1)).reshape(cols, features)
    gain = attention_norm_gain.astype(jnp.float32).reshape(PLANE, 1, width)
    anyspace = pl.BlockSpec(memory_space=pl.ANY)
    vmem = pl.BlockSpec(memory_space=pltpu.VMEM)
    dma = pltpu.SemaphoreType.DMA
    return pl.pallas_call(
        functools.partial(kernel, replicas, inner, planes, stored, rank),
        out_shape=jax.ShapeDtypeStruct((rows, outputs), jnp.bfloat16),
        in_specs=[anyspace, vmem, anyspace, anyspace, vmem, vmem],
        out_specs=vmem,
        scratch_shapes=[
            pltpu.VMEM((rows, outputs), jnp.float32),
            pltpu.VMEM((rows, 128), jnp.float32),
            pltpu.VMEM((PLANE, adapter_ids.shape[0], 16, rows), jnp.bfloat16),
            pltpu.VMEM((rows, features), jnp.bfloat16),
            pltpu.VMEM((features, outputs), jnp.bfloat16),
            pltpu.VMEM((planes, inner, cols, width), jnp.bfloat16),
            pltpu.VMEM((planes, inner, outputs // PLANE, cols), jnp.bfloat16),
            pltpu.VMEM((PLANE, rows, width), jnp.bfloat16),
            pltpu.VMEM((PLANE, 8, rows), jnp.int32),
            pltpu.VMEM((PLANE, rank, rows), jnp.float32),
            pltpu.VMEM((PLANE, rank, rows), jnp.float32),
            pltpu.VMEM((PLANE, rank, rows), jnp.bfloat16),
            pltpu.VMEM((PLANE, outputs // PLANE, rows), jnp.bfloat16),
            pltpu.VMEM((PLANE, outputs // PLANE, rows), jnp.bfloat16),
            dma((planes, inner)),
            dma((planes, inner)),
            dma((planes, inner)),
            dma((planes, inner)),
            dma((inner,)),
            dma((planes, inner)),
            dma((planes, inner)),
            dma((inner,)),
            dma((PLANE,)),
            dma((PLANE,)),
            dma((PLANE,)),
            dma((PLANE,)),
            dma((PLANE,)),
            dma((PLANE,)),
            dma((PLANE,)),
            dma((PLANE,)),
            dma((PLANE,)),
            dma((PLANE,)),
            dma((4,)),
        ],
        compiler_params=pltpu.CompilerParams(
            collective_id=0, has_side_effects=True, vmem_limit_bytes=56 * 1024 * 1024
        ),
        cost_estimate=pl.CostEstimate(
            flops=12 * 10**9, bytes_accessed=250 * 10**6, transcendentals=0
        ),
    )(
        residual_rows,
        gain,
        value_base_weight,
        down,
        up,
        jnp.broadcast_to(slot[None, :], (8, rows)),
    )


def solution(mesh):
    return jax.shard_map(
        shards,
        mesh=mesh,
        in_specs=(
            P(("replica", "req"), None),
            P(),
            P(),
            P("req", None, None),
            P("req", None, None),
            P("replica"),
            P(("replica", "req")),
        ),
        out_specs=P(("replica", "req"), None),
        check_vma=False,
    )
```

```python
import functools

import jax
import jax.numpy as jnp
from jax import lax
from jax.experimental import pallas as pl
from jax.experimental.pallas import tpu as pltpu
from jax.sharding import PartitionSpec as P

MESH = pl.DeviceIdType.MESH
PLANE = 8


def kernel(
    replicas,
    inner,
    planes,
    stored,
    rank,
    x_hbm,
    gain_ref,
    base_w_hbm,
    down_hbm,
    up_ref,
    slot_ref,
    out_ref,
    base_ref,
    square,
    hot,
    x_v,
    w_v,
    down_buf,
    up_buf,
    rows_buf,
    slot_buf,
    acc,
    part_buf,
    shrink_buf,
    answer,
    delta_buf,
    down_recv,
    small_recv,
    small_up,
    small_dn,
    small_plane,
    up_send,
    dn_send,
    plane_send,
    rows_send,
    rows_recv,
    slot_send,
    slot_recv,
    part_send,
    part_recv,
    shrink_send,
    shrink_recv,
    delta_send,
    delta_recv,
    local_sem,
):
    r = lax.axis_index("replica")
    q = lax.axis_index("req")
    z = q // inner
    i = q % inner
    e = r * inner + i
    rows = x_hbm.shape[0]
    width = x_hbm.shape[1] // PLANE
    cols = stored * rank

    def peer(k):
        e2 = 0
        for bit in (1, 2, 4):
            own = (e // bit) % 2
            e2 += bit * (1 - own if k & bit else own)
        return e2, (e2 // inner, z * inner + lax.rem(e2, inner))

    has_up = z < planes - 1
    has_dn = z > 0
    above = (r, jnp.minimum(z + 1, planes - 1) * inner + i)
    below = (r, jnp.maximum(z - 1, 0) * inner + i)

    own_x = pltpu.make_async_copy(x_hbm, x_v, local_sem.at[0])
    own_w = pltpu.make_async_copy(base_w_hbm, w_v, local_sem.at[1])
    own_down = pltpu.make_async_copy(
        down_hbm.at[:, pl.ds(pl.multiple_of(e * width, width), width)],
        down_buf.at[z, i],
        local_sem.at[2],
    )
    own_down.start()
    own_x.start()

    barrier = pltpu.get_barrier_semaphore()
    for k in range(1, PLANE):
        pl.semaphore_signal(barrier, inc=1, device_id=peer(k)[1], device_id_type=MESH)

    @pl.when(has_up)
    def _():
        pl.semaphore_signal(barrier, inc=1, device_id=above, device_id_type=MESH)

    @pl.when(has_dn)
    def _():
        pl.semaphore_signal(barrier, inc=1, device_id=below, device_id_type=MESH)

    lines = jnp.where(has_up, 1, 0) + jnp.where(has_dn, 1, 0)
    pl.semaphore_wait(barrier, PLANE - 1 + lines)

    def plane_copy(k):
        i2 = lax.rem(i + k, inner)
        e2 = r * inner + i2
        return pltpu.make_async_remote_copy(
            src_ref=down_hbm.at[:, pl.ds(pl.multiple_of(e2 * width, width), width)],
            dst_ref=down_buf.at[z, i],
            send_sem=plane_send.at[k],
            recv_sem=down_recv.at[z, i],
            device_id=(r, z * inner + i2),
            device_id_type=MESH,
        )

    share = up_ref.shape[0] // PLANE

    def small_copy(k):
        i2 = lax.rem(i + k, inner)
        e2 = r * inner + i2
        return pltpu.make_async_remote_copy(
            src_ref=up_ref.at[pl.ds(pl.multiple_of(e2 * share, share), share)],
            dst_ref=up_buf.at[z, i],
            send_sem=small_plane.at[k],
            recv_sem=small_recv.at[z, i],
            device_id=(r, z * inner + i2),
            device_id_type=MESH,
        )

    def small_line(b, j, up):
        return pltpu.make_async_remote_copy(
            src_ref=up_buf.at[b, j],
            dst_ref=up_buf.at[b, j],
            send_sem=(small_up if up else small_dn).at[b, j],
            recv_sem=small_recv.at[b, j],
            device_id=above if up else below,
            device_id_type=MESH,
        )

    def rows_copy(k):
        e2, dev = peer(k)
        return pltpu.make_async_remote_copy(
            src_ref=x_hbm.at[:, pl.ds(pl.multiple_of(e2 * width, width), width)],
            dst_ref=rows_buf.at[e],
            send_sem=rows_send.at[k],
            recv_sem=rows_recv.at[e],
            device_id=dev,
            device_id_type=MESH,
        )

    def slot_copy(k):
        _, dev = peer(k)
        return pltpu.make_async_remote_copy(
            src_ref=slot_ref,
            dst_ref=slot_buf.at[e],
            send_sem=slot_send.at[k],
            recv_sem=slot_recv.at[e],
            device_id=dev,
            device_id_type=MESH,
        )

    def line_copy(b, j, up):
        return pltpu.make_async_remote_copy(
            src_ref=down_buf.at[b, j],
            dst_ref=down_buf.at[b, j],
            send_sem=(up_send if up else dn_send).at[b, j],
            recv_sem=down_recv.at[b, j],
            device_id=above if up else below,
            device_id_type=MESH,
        )

    def block_recv(b, j):
        pltpu.make_async_remote_copy(
            src_ref=down_buf.at[b, j],
            dst_ref=down_buf.at[b, j],
            send_sem=up_send.at[b, j],
            recv_sem=down_recv.at[b, j],
            device_id=above,
            device_id_type=MESH,
        ).wait_recv()
        small_line(b, j, True).wait_recv()

    def pass_on(b, j, up):
        @pl.when(has_up if up else has_dn)
        def _():
            line_copy(b, j, up).start()
            small_line(b, j, up).start()

    for k in range(1, inner):
        plane_copy(k).start()
        small_copy(k).start()
    up_buf[z, i] = up_ref[pl.ds(pl.multiple_of(e * share, share), share), :]
    own_down.wait()
    pass_on(z, i, True)
    pass_on(z, i, False)
    for k in range(1, PLANE):
        slot_copy(k).start()
    own_w.start()
    slot_buf[e] = slot_ref[...]
    for k in range(1, inner):
        j = lax.rem(i + k, inner)
        block_recv(z, j)
        pass_on(z, j, True)
        pass_on(z, j, False)

    for k in (1, 4, 5, 2, 3, 6, 7):
        rows_copy(k).start()

    own_x.wait()
    own_w.wait()
    base_ref[...] = jnp.zeros_like(base_ref)
    square[...] = jnp.zeros_like(square)

    def base_step(c):
        at = pl.multiple_of(c * width, width)
        wide = x_v[:, pl.ds(at, width)].astype(jnp.float32)
        square[...] += jnp.sum(wide * wide, axis=1, keepdims=True)
        scaled = (wide * gain_ref[c]).astype(jnp.bfloat16)
        x_v[:, pl.ds(at, width)] = scaled
        base_ref[...] += jnp.dot(
            scaled, w_v[pl.ds(at, width), :], preferred_element_type=jnp.float32
        )

    gain_own = gain_ref[e]

    def multiply(n, down, first):
        product = lax.dot_general(
            down,
            rows_buf[n],
            (((1,), (1,)), ((), ())),
            preferred_element_type=jnp.float32,
        )
        slots = slot_buf[n][0:1, :]
        total = acc[n]
        for a in range(down.shape[0] // rank):
            total = jnp.where(slots == first + a, product[a * rank : (a + 1) * rank], total)
        acc[n] = total

    def multiply_row(n):
        @pl.loop(0, planes)
        def _(b):
            far = jnp.maximum(b - z, z - b)

            @pl.when(far < planes - 1)
            def _():
                multiply(n, down_buf[b].reshape(inner * cols, width), b * inner * stored)

    def multiply_last(b):
        @pl.loop(0, inner)
        def _(j):
            block_recv(b, j)

        @pl.loop(0, PLANE)
        def _(n):
            multiply(n, down_buf[b].reshape(inner * cols, width), b * inner * stored)

    @pl.loop(0, (planes - 2) * inner)
    def _(t):
        s = t // inner + 1
        j = (i + t) % inner

        @pl.when(z - s >= 0)
        def _():
            block_recv(z - s, j)
            pass_on(z - s, j, True)

        @pl.when(z + s < planes)
        def _():
            block_recv(z + s, j)
            pass_on(z + s, j, False)

        @pl.when(t < PLANE)
        def _():
            base_step(t)

    @pl.loop(min((planes - 2) * inner, PLANE), PLANE)
    def _(c):
        base_step(c)

    factor = lax.rsqrt(square[...] / (width * PLANE) + 1e-05)
    base_ref[...] = base_ref[...] * factor[:, 0:1]
    factor_row = jnp.transpose(factor)[0:1, :]

    own_rows = pltpu.make_async_copy(
        x_v.at[:, pl.ds(pl.multiple_of(e * width, width), width)],
        rows_buf.at[e],
        local_sem.at[3],
    )
    own_rows.start()
    acc[...] = jnp.zeros_like(acc)
    for k in range(1, PLANE):
        e2, dev = peer(k)
        pltpu.make_async_remote_copy(
            src_ref=slot_ref,
            dst_ref=slot_buf.at[e2],
            send_sem=slot_send.at[k],
            recv_sem=slot_recv.at[e2],
            device_id=dev,
            device_id_type=MESH,
        ).wait_recv()

    @pl.loop(0, PLANE)
    def _(n):
        slots = jnp.broadcast_to(slot_buf[n][0:1, :], (16, rows))

        @pl.loop(0, planes * inner * stored)
        def _(a):
            hot[n, a] = jnp.where(slots == a, 1.0, 0.0).astype(jnp.bfloat16)

    own_rows.wait()
    multiply_row(e)
    for k in (1, 4, 5, 2, 3, 6, 7):
        e2, dev = peer(k)
        pltpu.make_async_remote_copy(
            src_ref=rows_buf.at[e2],
            dst_ref=rows_buf.at[e2],
            send_sem=rows_send.at[k],
            recv_sem=rows_recv.at[e2],
            device_id=dev,
            device_id_type=MESH,
        ).wait_recv()
        rows_buf[e2] = (rows_buf[e2].astype(jnp.float32) * gain_own).astype(jnp.bfloat16)
        multiply_row(e2)

    @pl.when(z == 0)
    def _():
        multiply_last(planes - 1)

    @pl.when(z == planes - 1)
    def _():
        multiply_last(0)

    def part_copy(k):
        e2, dev = peer(k)
        return pltpu.make_async_remote_copy(
            src_ref=acc.at[e2],
            dst_ref=part_buf.at[e],
            send_sem=part_send.at[k],
            recv_sem=part_recv.at[e],
            device_id=dev,
            device_id_type=MESH,
        )

    for k in range(1, PLANE):
        part_copy(k).start()
    total = acc[e]
    for k in range(1, PLANE):
        e2, dev = peer(k)
        pltpu.make_async_remote_copy(
            src_ref=part_buf.at[e2],
            dst_ref=part_buf.at[e2],
            send_sem=part_send.at[k],
            recv_sem=part_recv.at[e2],
            device_id=dev,
            device_id_type=MESH,
        ).wait_recv()
        total += part_buf[e2]
    shrink_buf[e] = (total * factor_row).astype(jnp.bfloat16)

    def shrink_copy(k):
        _, dev = peer(k)
        return pltpu.make_async_remote_copy(
            src_ref=shrink_buf.at[e],
            dst_ref=shrink_buf.at[e],
            send_sem=shrink_send.at[k],
            recv_sem=shrink_recv.at[e],
            device_id=dev,
            device_id_type=MESH,
        )

    def delta_copy(k):
        e2, dev = peer(k)
        return pltpu.make_async_remote_copy(
            src_ref=answer.at[e2],
            dst_ref=delta_buf.at[e],
            send_sem=delta_send.at[k],
            recv_sem=delta_recv.at[e],
            device_id=dev,
            device_id_type=MESH,
        )

    def expand(n):
        shrunk = shrink_buf[n].reshape(rank // 16, 16, rows)

        def block(b, total):
            spread = jnp.concatenate(
                [
                    (shrunk * hot[n, b * inner * stored + a][None]).reshape(rank, rows)
                    for a in range(inner * stored)
                ],
                axis=0,
            )
            for j in range(inner):
                total += jnp.dot(
                    up_buf[b, j],
                    spread[j * cols : (j + 1) * cols],
                    preferred_element_type=jnp.float32,
                )
            return total

        zero = jnp.zeros((share, rows), jnp.float32)
        return lax.fori_loop(0, planes, block, zero).astype(jnp.bfloat16)

    for k in range(1, PLANE):
        shrink_copy(k).start()
    delta_buf[e] = expand(e)
    for k in range(1, PLANE):
        e2, dev = peer(k)
        pltpu.make_async_remote_copy(
            src_ref=shrink_buf.at[e2],
            dst_ref=shrink_buf.at[e2],
            send_sem=shrink_send.at[k],
            recv_sem=shrink_recv.at[e2],
            device_id=dev,
            device_id_type=MESH,
        ).wait_recv()
        answer[e2] = expand(e2)
        delta_copy(k).start()
    for k in range(1, PLANE):
        e2, dev = peer(k)
        pltpu.make_async_remote_copy(
            src_ref=delta_buf.at[e2],
            dst_ref=delta_buf.at[e2],
            send_sem=delta_send.at[k],
            recv_sem=delta_recv.at[e2],
            device_id=dev,
            device_id_type=MESH,
        ).wait_recv()
    delta = delta_buf[...].reshape(PLANE * share, rows).astype(jnp.float32)
    out_ref[...] = (base_ref[...] + jnp.transpose(delta)).astype(jnp.bfloat16)

    for k in range(1, inner):
        plane_copy(k).wait_send()
        small_copy(k).wait_send()
    for k in range(1, PLANE):
        slot_copy(k).wait_send()
        rows_copy(k).wait_send()
        part_copy(k).wait_send()
        shrink_copy(k).wait_send()
        delta_copy(k).wait_send()

    @pl.loop(0, planes)
    def _(b):
        @pl.when(jnp.logical_and(has_up, b <= z))
        def _():
            @pl.loop(0, inner)
            def _(j):
                line_copy(b, j, True).wait_send()
                small_line(b, j, True).wait_send()

        @pl.when(jnp.logical_and(has_dn, b >= z))
        def _():
            @pl.loop(0, inner)
            def _(j):
                line_copy(b, j, False).wait_send()
                small_line(b, j, False).wait_send()


def shards(
    residual_rows,
    attention_norm_gain,
    value_base_weight,
    adapter_down_weight,
    adapter_up_weight,
    adapter_storage_slot,
    request_adapter_index,
):
    replicas = lax.axis_size("replica")
    devices = lax.axis_size("req")
    inner = PLANE // replicas
    planes = devices // inner
    rows, features = residual_rows.shape
    width = features // PLANE
    stored, _, rank = adapter_down_weight.shape
    outputs = value_base_weight.shape[1]
    cols = stored * rank
    adapter_ids = jnp.arange(adapter_storage_slot.shape[0], dtype=jnp.int32)
    slot_hot = request_adapter_index[:, None] == adapter_ids[None, :]
    slot = jnp.sum(jnp.where(slot_hot, adapter_storage_slot[None, :], 0), axis=1)
    up = jnp.transpose(adapter_up_weight, (2, 0, 1)).reshape(outputs, cols)
    down = jnp.transpose(adapter_down_weight, (0, 2, 1)).reshape(cols, features)
    gain = attention_norm_gain.astype(jnp.float32).reshape(PLANE, 1, width)
    anyspace = pl.BlockSpec(memory_space=pl.ANY)
    vmem = pl.BlockSpec(memory_space=pltpu.VMEM)
    dma = pltpu.SemaphoreType.DMA
    return pl.pallas_call(
        functools.partial(kernel, replicas, inner, planes, stored, rank),
        out_shape=jax.ShapeDtypeStruct((rows, outputs), jnp.bfloat16),
        in_specs=[anyspace, vmem, anyspace, anyspace, vmem, vmem],
        out_specs=vmem,
        scratch_shapes=[
            pltpu.VMEM((rows, outputs), jnp.float32),
            pltpu.VMEM((rows, 128), jnp.float32),
            pltpu.VMEM((PLANE, adapter_ids.shape[0], 16, rows), jnp.bfloat16),
            pltpu.VMEM((rows, features), jnp.bfloat16),
            pltpu.VMEM((features, outputs), jnp.bfloat16),
            pltpu.VMEM((planes, inner, cols, width), jnp.bfloat16),
            pltpu.VMEM((planes, inner, outputs // PLANE, cols), jnp.bfloat16),
            pltpu.VMEM((PLANE, rows, width), jnp.bfloat16),
            pltpu.VMEM((PLANE, 8, rows), jnp.int32),
            pltpu.VMEM((PLANE, rank, rows), jnp.float32),
            pltpu.VMEM((PLANE, rank, rows), jnp.float32),
            pltpu.VMEM((PLANE, rank, rows), jnp.bfloat16),
            pltpu.VMEM((PLANE, outputs // PLANE, rows), jnp.bfloat16),
            pltpu.VMEM((PLANE, outputs // PLANE, rows), jnp.bfloat16),
            dma((planes, inner)),
            dma((planes, inner)),
            dma((planes, inner)),
            dma((planes, inner)),
            dma((inner,)),
            dma((planes, inner)),
            dma((planes, inner)),
            dma((inner,)),
            dma((PLANE,)),
            dma((PLANE,)),
            dma((PLANE,)),
            dma((PLANE,)),
            dma((PLANE,)),
            dma((PLANE,)),
            dma((PLANE,)),
            dma((PLANE,)),
            dma((PLANE,)),
            dma((PLANE,)),
            dma((4,)),
        ],
        compiler_params=pltpu.CompilerParams(
            collective_id=0, has_side_effects=True, vmem_limit_bytes=56 * 1024 * 1024
        ),
        cost_estimate=pl.CostEstimate(
            flops=12 * 10**9, bytes_accessed=250 * 10**6, transcendentals=0
        ),
    )(
        residual_rows,
        gain,
        value_base_weight,
        down,
        up,
        jnp.broadcast_to(slot[None, :], (8, rows)),
    )


def solution(mesh):
    return jax.shard_map(
        shards,
        mesh=mesh,
        in_specs=(
            P(("replica", "req"), None),
            P(),
            P(),
            P("req", None, None),
            P("req", None, None),
            P("replica"),
            P(("replica", "req")),
        ),
        out_specs=P(("replica", "req"), None),
        check_vma=False,
    )
```

```python
import functools

import jax
import jax.numpy as jnp
from jax import lax
from jax.experimental import pallas as pl
from jax.experimental.pallas import tpu as pltpu
from jax.sharding import PartitionSpec as P

MESH = pl.DeviceIdType.MESH
PLANE = 8


def kernel(
    replicas,
    inner,
    planes,
    stored,
    rank,
    x_hbm,
    gain_ref,
    base_w_hbm,
    down_hbm,
    up_ref,
    slot_ref,
    out_ref,
    base_ref,
    square,
    hot,
    x_v,
    w_v,
    down_buf,
    up_buf,
    rows_buf,
    slot_buf,
    acc,
    part_buf,
    shrink_buf,
    answer,
    delta_buf,
    down_recv,
    small_recv,
    small_up,
    small_dn,
    small_plane,
    up_send,
    dn_send,
    plane_send,
    rows_send,
    rows_recv,
    slot_send,
    slot_recv,
    part_send,
    part_recv,
    shrink_send,
    shrink_recv,
    delta_send,
    delta_recv,
    local_sem,
):
    r = lax.axis_index("replica")
    q = lax.axis_index("req")
    z = q // inner
    i = q % inner
    e = r * inner + i
    rows = x_hbm.shape[0]
    width = x_hbm.shape[1] // PLANE
    cols = stored * rank

    def peer(k):
        e2 = 0
        for bit in (1, 2, 4):
            own = (e // bit) % 2
            e2 += bit * (1 - own if k & bit else own)
        return e2, (e2 // inner, z * inner + lax.rem(e2, inner))

    has_up = z < planes - 1
    has_dn = z > 0
    above = (r, jnp.minimum(z + 1, planes - 1) * inner + i)
    below = (r, jnp.maximum(z - 1, 0) * inner + i)

    own_x = pltpu.make_async_copy(x_hbm, x_v, local_sem.at[0])
    own_w = pltpu.make_async_copy(base_w_hbm, w_v, local_sem.at[1])
    own_down = pltpu.make_async_copy(
        down_hbm.at[:, pl.ds(pl.multiple_of(e * width, width), width)],
        down_buf.at[z, i],
        local_sem.at[2],
    )
    own_down.start()
    own_x.start()

    barrier = pltpu.get_barrier_semaphore()
    for k in range(1, PLANE):
        pl.semaphore_signal(barrier, inc=1, device_id=peer(k)[1], device_id_type=MESH)

    @pl.when(has_up)
    def _():
        pl.semaphore_signal(barrier, inc=1, device_id=above, device_id_type=MESH)

    @pl.when(has_dn)
    def _():
        pl.semaphore_signal(barrier, inc=1, device_id=below, device_id_type=MESH)

    lines = jnp.where(has_up, 1, 0) + jnp.where(has_dn, 1, 0)
    pl.semaphore_wait(barrier, PLANE - 1 + lines)

    def plane_copy(k):
        i2 = lax.rem(i + k, inner)
        e2 = r * inner + i2
        return pltpu.make_async_remote_copy(
            src_ref=down_hbm.at[:, pl.ds(pl.multiple_of(e2 * width, width), width)],
            dst_ref=down_buf.at[z, i],
            send_sem=plane_send.at[k],
            recv_sem=down_recv.at[z, i],
            device_id=(r, z * inner + i2),
            device_id_type=MESH,
        )

    share = up_ref.shape[0] // PLANE

    def small_copy(k):
        i2 = lax.rem(i + k, inner)
        e2 = r * inner + i2
        return pltpu.make_async_remote_copy(
            src_ref=up_ref.at[pl.ds(pl.multiple_of(e2 * share, share), share)],
            dst_ref=up_buf.at[z, i],
            send_sem=small_plane.at[k],
            recv_sem=small_recv.at[z, i],
            device_id=(r, z * inner + i2),
            device_id_type=MESH,
        )

    def small_line(b, j, up):
        return pltpu.make_async_remote_copy(
            src_ref=up_buf.at[b, j],
            dst_ref=up_buf.at[b, j],
            send_sem=(small_up if up else small_dn).at[b, j],
            recv_sem=small_recv.at[b, j],
            device_id=above if up else below,
            device_id_type=MESH,
        )

    def rows_copy(k):
        e2, dev = peer(k)
        return pltpu.make_async_remote_copy(
            src_ref=x_hbm.at[:, pl.ds(pl.multiple_of(e2 * width, width), width)],
            dst_ref=rows_buf.at[e],
            send_sem=rows_send.at[k],
            recv_sem=rows_recv.at[e],
            device_id=dev,
            device_id_type=MESH,
        )

    def slot_copy(k):
        _, dev = peer(k)
        return pltpu.make_async_remote_copy(
            src_ref=slot_ref,
            dst_ref=slot_buf.at[e],
            send_sem=slot_send.at[k],
            recv_sem=slot_recv.at[e],
            device_id=dev,
            device_id_type=MESH,
        )

    def line_copy(b, j, up):
        return pltpu.make_async_remote_copy(
            src_ref=down_buf.at[b, j],
            dst_ref=down_buf.at[b, j],
            send_sem=(up_send if up else dn_send).at[b, j],
            recv_sem=down_recv.at[b, j],
            device_id=above if up else below,
            device_id_type=MESH,
        )

    def block_recv(b, j):
        pltpu.make_async_remote_copy(
            src_ref=down_buf.at[b, j],
            dst_ref=down_buf.at[b, j],
            send_sem=up_send.at[b, j],
            recv_sem=down_recv.at[b, j],
            device_id=above,
            device_id_type=MESH,
        ).wait_recv()
        small_line(b, j, True).wait_recv()

    def pass_on(b, j, up):
        @pl.when(has_up if up else has_dn)
        def _():
            line_copy(b, j, up).start()
            small_line(b, j, up).start()

    for k in range(1, inner):
        plane_copy(k).start()
        small_copy(k).start()
    up_buf[z, i] = up_ref[pl.ds(pl.multiple_of(e * share, share), share), :]
    own_down.wait()
    pass_on(z, i, True)
    pass_on(z, i, False)
    for k in range(1, PLANE):
        slot_copy(k).start()
    own_w.start()
    slot_buf[e] = slot_ref[...]
    for k in range(1, inner):
        j = lax.rem(i + k, inner)
        block_recv(z, j)
        pass_on(z, j, True)
        pass_on(z, j, False)

    for k in (6, 7, 2, 3, 4, 5, 1):
        rows_copy(k).start()

    own_x.wait()
    own_w.wait()
    base_ref[...] = jnp.zeros_like(base_ref)
    square[...] = jnp.zeros_like(square)

    def base_step(c):
        at = pl.multiple_of(c * width, width)
        wide = x_v[:, pl.ds(at, width)].astype(jnp.float32)
        square[...] += jnp.sum(wide * wide, axis=1, keepdims=True)
        scaled = (wide * gain_ref[c]).astype(jnp.bfloat16)
        x_v[:, pl.ds(at, width)] = scaled
        base_ref[...] += jnp.dot(
            scaled, w_v[pl.ds(at, width), :], preferred_element_type=jnp.float32
        )

    gain_own = gain_ref[e]

    def multiply(n, down, first):
        product = lax.dot_general(
            down,
            rows_buf[n],
            (((1,), (1,)), ((), ())),
            preferred_element_type=jnp.float32,
        )
        slots = slot_buf[n][0:1, :]
        total = acc[n]
        for a in range(down.shape[0] // rank):
            total = jnp.where(slots == first + a, product[a * rank : (a + 1) * rank], total)
        acc[n] = total

    def multiply_row(n):
        @pl.loop(0, planes)
        def _(b):
            far = jnp.maximum(b - z, z - b)

            @pl.when(far < planes - 1)
            def _():
                multiply(n, down_buf[b].reshape(inner * cols, width), b * inner * stored)

    def multiply_last(b):
        @pl.loop(0, inner)
        def _(j):
            block_recv(b, j)

        @pl.loop(0, PLANE)
        def _(n):
            multiply(n, down_buf[b].reshape(inner * cols, width), b * inner * stored)

    @pl.loop(0, (planes - 2) * inner)
    def _(t):
        s = t // inner + 1
        j = (i + t) % inner

        @pl.when(z - s >= 0)
        def _():
            block_recv(z - s, j)
            pass_on(z - s, j, True)

        @pl.when(z + s < planes)
        def _():
            block_recv(z + s, j)
            pass_on(z + s, j, False)

        @pl.when(t < PLANE)
        def _():
            base_step(t)

    @pl.loop(min((planes - 2) * inner, PLANE), PLANE)
    def _(c):
        base_step(c)

    factor = lax.rsqrt(square[...] / (width * PLANE) + 1e-05)
    base_ref[...] = base_ref[...] * factor[:, 0:1]
    factor_row = jnp.transpose(factor)[0:1, :]

    own_rows = pltpu.make_async_copy(
        x_v.at[:, pl.ds(pl.multiple_of(e * width, width), width)],
        rows_buf.at[e],
        local_sem.at[3],
    )
    own_rows.start()
    acc[...] = jnp.zeros_like(acc)
    for k in range(1, PLANE):
        e2, dev = peer(k)
        pltpu.make_async_remote_copy(
            src_ref=slot_ref,
            dst_ref=slot_buf.at[e2],
            send_sem=slot_send.at[k],
            recv_sem=slot_recv.at[e2],
            device_id=dev,
            device_id_type=MESH,
        ).wait_recv()

    @pl.loop(0, PLANE)
    def _(n):
        slots = jnp.broadcast_to(slot_buf[n][0:1, :], (16, rows))

        @pl.loop(0, planes * inner * stored)
        def _(a):
            hot[n, a] = jnp.where(slots == a, 1.0, 0.0).astype(jnp.bfloat16)

    own_rows.wait()
    multiply_row(e)
    for k in (1, 4, 5, 2, 3, 6, 7):
        e2, dev = peer(k)
        pltpu.make_async_remote_copy(
            src_ref=rows_buf.at[e2],
            dst_ref=rows_buf.at[e2],
            send_sem=rows_send.at[k],
            recv_sem=rows_recv.at[e2],
            device_id=dev,
            device_id_type=MESH,
        ).wait_recv()
        rows_buf[e2] = (rows_buf[e2].astype(jnp.float32) * gain_own).astype(jnp.bfloat16)
        multiply_row(e2)

    @pl.when(z == 0)
    def _():
        multiply_last(planes - 1)

    @pl.when(z == planes - 1)
    def _():
        multiply_last(0)

    def part_copy(k):
        e2, dev = peer(k)
        return pltpu.make_async_remote_copy(
            src_ref=acc.at[e2],
            dst_ref=part_buf.at[e],
            send_sem=part_send.at[k],
            recv_sem=part_recv.at[e],
            device_id=dev,
            device_id_type=MESH,
        )

    for k in range(1, PLANE):
        part_copy(k).start()
    total = acc[e]
    for k in range(1, PLANE):
        e2, dev = peer(k)
        pltpu.make_async_remote_copy(
            src_ref=part_buf.at[e2],
            dst_ref=part_buf.at[e2],
            send_sem=part_send.at[k],
            recv_sem=part_recv.at[e2],
            device_id=dev,
            device_id_type=MESH,
        ).wait_recv()
        total += part_buf[e2]
    shrink_buf[e] = (total * factor_row).astype(jnp.bfloat16)

    def shrink_copy(k):
        _, dev = peer(k)
        return pltpu.make_async_remote_copy(
            src_ref=shrink_buf.at[e],
            dst_ref=shrink_buf.at[e],
            send_sem=shrink_send.at[k],
            recv_sem=shrink_recv.at[e],
            device_id=dev,
            device_id_type=MESH,
        )

    def delta_copy(k):
        e2, dev = peer(k)
        return pltpu.make_async_remote_copy(
            src_ref=answer.at[e2],
            dst_ref=delta_buf.at[e],
            send_sem=delta_send.at[k],
            recv_sem=delta_recv.at[e],
            device_id=dev,
            device_id_type=MESH,
        )

    def expand(n):
        shrunk = shrink_buf[n].reshape(rank // 16, 16, rows)

        def block(b, total):
            spread = jnp.concatenate(
                [
                    (shrunk * hot[n, b * inner * stored + a][None]).reshape(rank, rows)
                    for a in range(inner * stored)
                ],
                axis=0,
            )
            for j in range(inner):
                total += jnp.dot(
                    up_buf[b, j],
                    spread[j * cols : (j + 1) * cols],
                    preferred_element_type=jnp.float32,
                )
            return total

        zero = jnp.zeros((share, rows), jnp.float32)
        return lax.fori_loop(0, planes, block, zero).astype(jnp.bfloat16)

    for k in range(1, PLANE):
        shrink_copy(k).start()
    delta_buf[e] = expand(e)
    for k in range(1, PLANE):
        e2, dev = peer(k)
        pltpu.make_async_remote_copy(
            src_ref=shrink_buf.at[e2],
            dst_ref=shrink_buf.at[e2],
            send_sem=shrink_send.at[k],
            recv_sem=shrink_recv.at[e2],
            device_id=dev,
            device_id_type=MESH,
        ).wait_recv()
        answer[e2] = expand(e2)
        delta_copy(k).start()
    for k in range(1, PLANE):
        e2, dev = peer(k)
        pltpu.make_async_remote_copy(
            src_ref=delta_buf.at[e2],
            dst_ref=delta_buf.at[e2],
            send_sem=delta_send.at[k],
            recv_sem=delta_recv.at[e2],
            device_id=dev,
            device_id_type=MESH,
        ).wait_recv()
    delta = delta_buf[...].reshape(PLANE * share, rows).astype(jnp.float32)
    out_ref[...] = (base_ref[...] + jnp.transpose(delta)).astype(jnp.bfloat16)

    for k in range(1, inner):
        plane_copy(k).wait_send()
        small_copy(k).wait_send()
    for k in range(1, PLANE):
        slot_copy(k).wait_send()
        rows_copy(k).wait_send()
        part_copy(k).wait_send()
        shrink_copy(k).wait_send()
        delta_copy(k).wait_send()

    @pl.loop(0, planes)
    def _(b):
        @pl.when(jnp.logical_and(has_up, b <= z))
        def _():
            @pl.loop(0, inner)
            def _(j):
                line_copy(b, j, True).wait_send()
                small_line(b, j, True).wait_send()

        @pl.when(jnp.logical_and(has_dn, b >= z))
        def _():
            @pl.loop(0, inner)
            def _(j):
                line_copy(b, j, False).wait_send()
                small_line(b, j, False).wait_send()


def shards(
    residual_rows,
    attention_norm_gain,
    value_base_weight,
    adapter_down_weight,
    adapter_up_weight,
    adapter_storage_slot,
    request_adapter_index,
):
    replicas = lax.axis_size("replica")
    devices = lax.axis_size("req")
    inner = PLANE // replicas
    planes = devices // inner
    rows, features = residual_rows.shape
    width = features // PLANE
    stored, _, rank = adapter_down_weight.shape
    outputs = value_base_weight.shape[1]
    cols = stored * rank
    adapter_ids = jnp.arange(adapter_storage_slot.shape[0], dtype=jnp.int32)
    slot_hot = request_adapter_index[:, None] == adapter_ids[None, :]
    slot = jnp.sum(jnp.where(slot_hot, adapter_storage_slot[None, :], 0), axis=1)
    up = jnp.transpose(adapter_up_weight, (2, 0, 1)).reshape(outputs, cols)
    down = jnp.transpose(adapter_down_weight, (0, 2, 1)).reshape(cols, features)
    gain = attention_norm_gain.astype(jnp.float32).reshape(PLANE, 1, width)
    anyspace = pl.BlockSpec(memory_space=pl.ANY)
    vmem = pl.BlockSpec(memory_space=pltpu.VMEM)
    dma = pltpu.SemaphoreType.DMA
    return pl.pallas_call(
        functools.partial(kernel, replicas, inner, planes, stored, rank),
        out_shape=jax.ShapeDtypeStruct((rows, outputs), jnp.bfloat16),
        in_specs=[anyspace, vmem, anyspace, anyspace, vmem, vmem],
        out_specs=vmem,
        scratch_shapes=[
            pltpu.VMEM((rows, outputs), jnp.float32),
            pltpu.VMEM((rows, 128), jnp.float32),
            pltpu.VMEM((PLANE, adapter_ids.shape[0], 16, rows), jnp.bfloat16),
            pltpu.VMEM((rows, features), jnp.bfloat16),
            pltpu.VMEM((features, outputs), jnp.bfloat16),
            pltpu.VMEM((planes, inner, cols, width), jnp.bfloat16),
            pltpu.VMEM((planes, inner, outputs // PLANE, cols), jnp.bfloat16),
            pltpu.VMEM((PLANE, rows, width), jnp.bfloat16),
            pltpu.VMEM((PLANE, 8, rows), jnp.int32),
            pltpu.VMEM((PLANE, rank, rows), jnp.float32),
            pltpu.VMEM((PLANE, rank, rows), jnp.float32),
            pltpu.VMEM((PLANE, rank, rows), jnp.bfloat16),
            pltpu.VMEM((PLANE, outputs // PLANE, rows), jnp.bfloat16),
            pltpu.VMEM((PLANE, outputs // PLANE, rows), jnp.bfloat16),
            dma((planes, inner)),
            dma((planes, inner)),
            dma((planes, inner)),
            dma((planes, inner)),
            dma((inner,)),
            dma((planes, inner)),
            dma((planes, inner)),
            dma((inner,)),
            dma((PLANE,)),
            dma((PLANE,)),
            dma((PLANE,)),
            dma((PLANE,)),
            dma((PLANE,)),
            dma((PLANE,)),
            dma((PLANE,)),
            dma((PLANE,)),
            dma((PLANE,)),
            dma((PLANE,)),
            dma((4,)),
        ],
        compiler_params=pltpu.CompilerParams(
            collective_id=0, has_side_effects=True, vmem_limit_bytes=56 * 1024 * 1024
        ),
        cost_estimate=pl.CostEstimate(
            flops=12 * 10**9, bytes_accessed=250 * 10**6, transcendentals=0
        ),
    )(
        residual_rows,
        gain,
        value_base_weight,
        down,
        up,
        jnp.broadcast_to(slot[None, :], (8, rows)),
    )


def solution(mesh):
    return jax.shard_map(
        shards,
        mesh=mesh,
        in_specs=(
            P(("replica", "req"), None),
            P(),
            P(),
            P("req", None, None),
            P("req", None, None),
            P("replica"),
            P(("replica", "req")),
        ),
        out_specs=P(("replica", "req"), None),
        check_vma=False,
    )
```
